256 devices in a mesh: gx: 16 (over z_hi, y), gy: 8 (over x, core), gz: 2 (over z_lo).
Axes of the slice: x: 4, y: 4, z: 8 (z_hi: 4, z_lo: 2; z = z_hi * 2 + z_lo), core: 2. Of those that a mesh axis runs over, the one named last changes fastest.
Arguments:
- weights: float32 [2, 27, 16, 16, 2, 8, 256], P(None, None, 'gx', 'gy', 'gz'), may hold values from -0.3 to 0.3
- target_box: int32 [3, 256], replicated, may hold values from 0 to 15
- wave_speed: float32 [256], replicated, may hold values from 0.15 to 0.6
Outputs:
- level_six: float32 [2, 27, 2, 256, 2048], P(None, None, 'gz', ('gx', 'gy'))
The draws below stay inside these ranges and needn't reach their ends.
All inputs are finite; a program needn't handle non-finite values.
Results may differ from the reference program's by a relative error of at most 0.0003.
Values sent between devices are 32-bit elements; how exact they have to be, the bound alone decides.
A program may use at most 128 MiB of HBM per device.

```python
import math
import jax
import jax.numpy as jnp
import numpy as np
from jax import lax

TG = 16
NK = 256
SZ = 16
SX = 16
SY = 16
ZH = 8
TW = 256
QX = 4
QY = 4
QZ = 4
COLS = 2048


def set_ends(drawn, rng, low, largest):
    index_at = [jax.random.randint(jax.random.fold_in(rng, axis), (), 0, length) for axis, length in enumerate(drawn.shape)]
    longest = drawn.shape.index(max(drawn.shape))
    beside = index_at[:longest] + [(index_at[longest] + 1) % drawn.shape[longest]] + index_at[longest + 1:]
    return drawn.at[tuple(index_at)].set(low).at[tuple(beside)].set(largest)


def level_of(stream_key, shape, shards, smallest, largest):
    loudness, own = 1.0, jax.random.fold_in(stream_key, 6)
    for position, blocks in shards:
        heights = jnp.exp(jax.random.uniform(jax.random.fold_in(own, position), (blocks,), jnp.float32, smallest / len(shards), largest / len(shards)))
        loudness = loudness * jnp.repeat(heights, shape[position] // blocks).reshape([-1 if axis == position else 1 for axis in range(len(shape))])
    return loudness


def normal_values(rng, dims, spread, limit, pieces=(), held_as=jnp.bfloat16):
    values = jax.random.normal(rng, dims, jnp.float32) * spread
    if len(pieces) > 0:
        values = level_of(rng, dims, pieces, -0.22, 0.18) * values
    return jnp.clip(values, min=-limit, max=limit).astype(held_as)


def setup_inputs(seed: int = 0) -> dict:
    key_list = jax.random.split(jax.random.key(seed), 4)
    return {
        "weights": normal_values(key_list[0], (2, 27, SX, SY, 2, ZH, TW), 0.05, 0.3, ((2, 16), (3, 8), (4, 2)), jnp.float32),
        "target_box": set_ends(jax.random.randint(key_list[1], (3, TW), 0, TG), jax.random.fold_in(key_list[1], 1), 0, TG - 1).astype(jnp.int32),
        "wave_speed": jnp.clip(jnp.exp(jax.random.uniform(key_list[2], (TW,), jnp.float32, math.log(0.15), math.log(0.6))), 0.15, 0.6),
    }


def chebyshev_points():
    return np.array([-math.sqrt(3.0) / 2.0, 0.0, math.sqrt(3.0) / 2.0])

def node_places():
    points = chebyshev_points()
    numbers = np.arange(27)
    return (points[numbers // 9], points[numbers // 3 % 3], points[numbers % 3])

def lagrange_line(child_bit):
    points = chebyshev_points()
    places = child_bit - 0.5 + points / 2.0
    lagrange = np.ones((3, 3))
    for parent_node in range(3):
        for others in range(3):
            if others != parent_node:
                lagrange[parent_node, :] = lagrange[parent_node, :] * (places - points[others]) / (points[parent_node] - points[others])
    return lagrange

def child_bits(child_code):
    return (child_code // 4, child_code // 2 % 2, child_code % 2)

def child_matrix(child_code):
    picked = child_bits(child_code)
    return np.kron(np.kron(lagrange_line(picked[0]), lagrange_line(picked[1])), lagrange_line(picked[2]))

def merge_matrix():
    return jnp.asarray(np.concatenate([child_matrix(child_code) for child_code in range(8)], axis=1), jnp.float32)

def switch_matrix(factors):
    places = node_places()
    turned = np.zeros((27, 27))
    for axis_number in range(3):
        turned = turned + factors[axis_number] * np.outer(places[axis_number], places[axis_number])
    turned = 2.0 * math.pi * turned
    cosine = np.cos(turned)
    sine_part = np.sin(turned)
    upper = np.concatenate([cosine, -sine_part], axis=1)
    lower = np.concatenate([sine_part, cosine], axis=1)
    joined = np.concatenate([upper, lower], axis=0)
    return jnp.asarray(joined.reshape(2, 27, 2, 27), jnp.float32)

def shaped_nodes(trailing):
    return tuple((jnp.asarray(coords, jnp.float32).reshape((27,) + (1,) * trailing) for coords in node_places()))

def box_centers(number, spacing):
    return -NK / 2.0 + (jnp.arange(number, dtype=jnp.float32) + 0.5) * spacing

def relative_phase(place, speeds, freq, step):
    anchor = jnp.sqrt(freq[0] * freq[0] + freq[1] * freq[1] + freq[2] * freq[2])
    shifted = jnp.sqrt((freq[0] + step[0]) * (freq[0] + step[0]) + (freq[1] + step[1]) * (freq[1] + step[1]) + (freq[2] + step[2]) * (freq[2] + step[2]))
    growth = (step[0] * (2.0 * freq[0] + step[0]) + step[1] * (2.0 * freq[1] + step[1]) + step[2] * (2.0 * freq[2] + step[2])) / (shifted + anchor)
    return 2.0 * math.pi * (place[0] * step[0] + place[1] * step[1] + place[2] * step[2] + speeds * growth)

def merge_level(children, place, speeds, freq, widths, node_axes):
    phased = []
    for child_code in range(8):
        picked = child_bits(child_code)
        step = tuple(((picked[axis_number] - 0.5) * widths[axis_number] + 0.5 * widths[axis_number] * node_axes[axis_number] for axis_number in range(3)))
        turned = relative_phase(place, speeds, freq, step)
        cosine = jnp.cos(turned)
        sine_part = jnp.sin(turned)
        real_part = children[child_code][0]
        imag_part = children[child_code][1]
        phased.append(jnp.stack([real_part * cosine - imag_part * sine_part, real_part * sine_part + imag_part * cosine]))
    stacked = jnp.concatenate(phased, axis=1)
    flattened = stacked.reshape(2, 216, -1)
    merged = jnp.einsum('tk,rkm->rtm', merge_matrix(), flattened, precision=lax.Precision.HIGHEST)
    return merged.reshape((2, 27) + stacked.shape[2:])

def apply_switch(merged, factors):
    flattened = merged.reshape(2, 27, -1)
    switched = jnp.einsum('atbs,bsm->atm', switch_matrix(factors), flattened, precision=lax.Precision.HIGHEST)
    return switched.reshape(merged.shape)

def window(portion, centers, speeds):
    targets = portion.shape[-1]
    target_four = 1.0 / TG
    target_five = target_four / 2.0
    target_six = target_five / 2.0
    widths_four = (NK / SX, NK / SY, NK / SZ)
    widths_five = tuple((2.0 * spacing for spacing in widths_four))
    widths_six = tuple((4.0 * spacing for spacing in widths_four))
    factors = tuple((target_five * spacing / 4.0 for spacing in widths_five))
    shaped = portion.reshape(2, 27, SX // 2, 2, SY // 2, 2, 2, ZH, targets)
    children = [shaped[:, :, :, child_bits(child_code)[0], :, child_bits(child_code)[1], child_bits(child_code)[2]] for child_code in range(8)]
    merge_nodes = shaped_nodes(4)
    freq_five = (box_centers(SX // 2, widths_five[0]).reshape(-1, 1, 1, 1), box_centers(SY // 2, widths_five[1]).reshape(-1, 1, 1), box_centers(ZH, widths_five[2]).reshape(-1, 1))
    later_nodes = shaped_nodes(7)
    freq_six = (box_centers(QX, widths_six[0]).reshape(-1, 1, 1, 1, 1, 1, 1), box_centers(QY, widths_six[1]).reshape(-1, 1, 1, 1, 1), box_centers(QZ, widths_six[2]).reshape(-1, 1, 1))
    halves = jnp.arange(2, dtype=jnp.float32) - 0.5
    later_step = ((halves * widths_five[0]).reshape(2, 1, 1, 1, 1, 1), (halves * widths_five[1]).reshape(2, 1, 1, 1), (halves * widths_five[2]).reshape(2, 1))
    layers = []
    for sigma_z in range(2):
        columns = []
        for sigma_x in range(2):
            rows_done = []
            for sigma_y in range(2):
                sigma = (sigma_x, sigma_y, sigma_z)
                place = tuple((centers[axis_number] + (sigma[axis_number] - 0.5) * target_four / 2.0 for axis_number in range(3)))
                merged = merge_level(children, place, speeds, freq_five, widths_four, merge_nodes)
                switched = apply_switch(merged, factors)
                grid = switched.reshape(2, 27, QX, 2, QY, 2, QZ, 2, targets)
                flattened = grid.reshape(2, 27, -1)
                outputs = []
                for tau_code in range(8):
                    tau = child_bits(tau_code)
                    node_place = tuple((place[axis_number] + (tau[axis_number] - 0.5) * target_five / 2.0 + target_six / 2.0 * later_nodes[axis_number] for axis_number in range(3)))
                    moved = jnp.einsum('kt,rkm->rtm', jnp.asarray(child_matrix(tau_code), jnp.float32), flattened, precision=lax.Precision.HIGHEST).reshape(grid.shape)
                    turned = relative_phase(node_place, speeds, freq_six, later_step)
                    cosine = jnp.cos(turned)
                    sine_part = jnp.sin(turned)
                    real_part = lax.optimization_barrier(jnp.sum(moved[0] * cosine - moved[1] * sine_part, axis=(2, 4, 6)))
                    imag_part = lax.optimization_barrier(jnp.sum(moved[0] * sine_part + moved[1] * cosine, axis=(2, 4, 6)))
                    outputs.append(jnp.stack([real_part, imag_part]))
                rows_done.append(jnp.stack(outputs, axis=2))
            columns.append(jnp.stack(rows_done, axis=2))
        layers.append(jnp.stack(columns, axis=2))
    result = jnp.stack(layers, axis=2)
    result = jnp.moveaxis(result, -1, 3)
    return result.reshape(2, 27, 2, targets, COLS)

def reference(weights, target_box, wave_speed):
    block_size = 16
    centers = (target_box.astype(jnp.float32) + 0.5) / TG - 0.5

    def one_block(number):
        offset = number * block_size
        portion = lax.dynamic_slice_in_dim(weights, offset, block_size, 6)
        block_centers = lax.dynamic_slice_in_dim(centers, offset, block_size, 1)
        speeds = lax.dynamic_slice_in_dim(wave_speed, offset, block_size, 0)
        return window(portion, block_centers, speeds)
    blocks = lax.map(one_block, jnp.arange(TW // block_size, dtype=jnp.int32))
    blocks = jnp.transpose(blocks, (1, 2, 3, 0, 4, 5))
    return blocks.reshape(2, 27, 2, TW, COLS)
```

```python
import functools
import math

import jax
import jax.numpy as jnp
import numpy as np
from jax import lax
from jax.experimental import pallas as pl
from jax.experimental.pallas import tpu as pltpu
from jax.sharding import PartitionSpec as P

TG = 16
NK = 256.0
MESH = pl.DeviceIdType.MESH
F32 = jnp.float32
BF16 = jnp.bfloat16


def chebyshev_points():
    return np.array([-math.sqrt(3.0) / 2.0, 0.0, math.sqrt(3.0) / 2.0])


def node_places():
    points = chebyshev_points()
    numbers = np.arange(27)
    return np.stack([points[numbers // 9], points[numbers // 3 % 3], points[numbers % 3]])


def lagrange_line(child_bit):
    points = chebyshev_points()
    places = child_bit - 0.5 + points / 2.0
    lagrange = np.ones((3, 3))
    for parent_node in range(3):
        for others in range(3):
            if others != parent_node:
                lagrange[parent_node, :] = (
                    lagrange[parent_node, :]
                    * (places - points[others])
                    / (points[parent_node] - points[others])
                )
    return lagrange


def child_bits(code):
    return (code // 4, code // 2 % 2, code % 2)


def child_matrix(code):
    picked = child_bits(code)
    return np.kron(
        np.kron(lagrange_line(picked[0]), lagrange_line(picked[1])), lagrange_line(picked[2])
    )


W4 = NK / 16
W5, W6 = 2 * W4, 4 * W4
H4 = 1.0 / TG
H5, H6 = H4 / 2, H4 / 4


def signs(code):
    return np.array(child_bits(code)) - 0.5


def child_step(code):
    return signs(code)[:, None] * W4 + 0.5 * W4 * node_places()


def lane_of(code, part):
    bx, by, bz = child_bits(code)
    return (bx * 2 + bz) * 128 + part * 64 + 2 * np.arange(27) + by


@functools.cache
def tables():
    places = node_places()
    turn = np.exp(2j * math.pi * H5 * W5 / 4.0 * (places.T @ places))
    parity = {}
    for sigma in range(8):
        row = [np.exp(2j * math.pi * (signs(sigma) * H4 / 2) @ (signs(a) * W5)) for a in range(8)]
        parity[sigma] = np.array(row)
    along = parity[0] / parity[0][0]
    merge = np.zeros((2, 512, 2, 4, 32))
    for sigma in range(8):
        assert np.allclose(parity[sigma], parity[sigma][0] * along)
        for code in range(8):
            shift = np.exp(2j * math.pi * (signs(sigma) * H4 / 2) @ child_step(code))
            both = (turn @ child_matrix(code)) * shift[None, :] * parity[sigma][0] * -1.0
            half = merge[sigma % 2]
            real, imag = lane_of(code, 0), lane_of(code, 1)
            half[real, 0, sigma // 2, :27] = both.real.T
            half[real, 1, sigma // 2, :27] = both.imag.T
            half[imag, 0, sigma // 2, :27] = -both.imag.T
            half[imag, 1, sigma // 2, :27] = both.real.T
    merge = merge.reshape(2, 512, 256)
    later = np.zeros((2, 4, 56, 8, 2, 32))
    for tau in range(8):
        spot = (signs(tau) * H5 / 2)[:, None] + H6 / 2 * places
        for a in range(8):
            shift = np.exp(2j * math.pi * (signs(a) * W5) @ spot) * along[a]
            both = child_matrix(tau).T * shift[:, None]
            block = later[tau % 2, tau // 2]
            block[:27, a, 0, :27] = both.real
            block[:27, a, 1, :27] = -both.imag
            block[27:54, a, 0, :27] = both.imag
            block[27:54, a, 1, :27] = both.real
    later = later.reshape(448, 512)
    radius = np.zeros((2, 4, 2, 2, 2, 4, 2, 4, 128))
    steps = np.zeros((8, 4, 128))
    for code in range(8):
        bx, by, bz = child_bits(code)
        offset = child_step(code)
        for part in range(2):
            lanes = lane_of(code, part) % 128
            steps[:3, bx * 2 + bz, lanes] = offset
            for gz, qx, ax, qylo, ay, az, qz in np.ndindex(2, 4, 2, 2, 2, 2, 4):
                q = np.array([qx, 2 * ((gz + qx) % 2) + qylo, qz])
                center = -NK / 2 + (2 * q + np.array([ax, ay, az]) + 0.5) * W5
                anchor = -NK / 2 + (q + 0.5) * W6
                node = center[:, None] + offset
                radius[gz, qx, ax, qylo, ay, bx * 2 + bz, az, qz, lanes] = np.sqrt(
                    (node**2).sum(0)
                ) - np.sqrt((anchor**2).sum())
    steps[3, :, 64:] = -0.25
    return merge, later, radius.reshape(2, 32, 4, 8, 128), steps


@functools.cache
def cosine_terms():
    nodes = np.cos((np.arange(400) + 0.5) * math.pi / 400) * 0.125 + 0.125
    fitted = np.polynomial.Polynomial.fit(nodes, np.cos(2 * math.pi * np.sqrt(nodes)), 7)
    return [float(c) for c in fitted.convert().coef]


def cosine_of_turns(turns):
    turns = turns - jnp.round(turns)
    square = turns * turns
    terms = cosine_terms()
    total = terms[-1]
    for term in terms[-2::-1]:
        total = total * square + term
    return total


def halves_of(matrix):
    wide = np.asarray(matrix, np.float32)
    high = wide.astype(jnp.bfloat16)
    low = (wide - high.astype(np.float32)).astype(jnp.bfloat16)
    return high, low


def split(x):
    high = x.astype(BF16)
    return high, (x - high.astype(F32)).astype(BF16)


def dot3(a, b):
    out = jnp.dot(a[0], b[0], preferred_element_type=F32)
    out += jnp.dot(a[0], b[1], preferred_element_type=F32)
    return out + jnp.dot(a[1], b[0], preferred_element_type=F32)


def spread_kernel(w_ref, out_ref, taken, turned, chunks, take_sem, send_sem, recv_sem):
    gx, gy, gz = lax.axis_index("gx"), lax.axis_index("gy"), lax.axis_index("gz")
    takes = [
        pltpu.make_async_copy(
            w_ref.at[:, half * 128 : half * 128 + 128], taken.at[half], take_sem.at[half]
        )
        for half in range(2)
    ]
    for take in takes:
        take.start()
    turned[...] = jnp.zeros_like(turned)
    for half in range(2):
        takes[half].wait()
        for depth in range(8):
            turned[0:54, :] = taken.at[half][pl.ds(depth, 54, stride=8), :]
            turned[64:118, :] = taken.at[half][pl.ds(432 + depth, 54, stride=8), :]
            row = half * 1024 + depth % 2 * 4 + depth // 2
            chunks[pl.ds(row, 128, stride=8), :] = turned[...].T
    tile = ((gx // 2) * 2 + gy // 2 % 2) * 2 + gy % 2
    block = gx % 2 * 2 + gz
    layer = (gx // 4 + gy // 4) % 2
    inside = layer == gz
    mine = gx * 8 + gy

    @pl.when(inside)
    def _():
        pltpu.make_async_copy(
            chunks.at[pl.ds(pl.multiple_of(mine * 16, 16), 16)], out_ref.at[tile, block], recv_sem
        ).start()

    @pl.when(jnp.logical_not(inside))
    def _():
        pltpu.make_async_remote_copy(
            chunks.at[pl.ds(pl.multiple_of(mine * 16, 16), 16)],
            out_ref.at[tile, block],
            send_sem,
            recv_sem,
            device_id=(gx, gy, layer),
            device_id_type=MESH,
        ).start()

    def send(step, carry):
        to_z = (gx // 4 + step) % 4
        to_y = (gx + step // 16) % 4
        to_x = (gy // 2 + step // 4) % 4
        to_core = (gy + step // 64) % 2
        to_gx = to_z * 4 + to_y
        to_gy = to_x * 2 + to_core
        start = pl.multiple_of((to_gx * 8 + to_gy) * 16, 16)
        pltpu.make_async_remote_copy(
            chunks.at[pl.ds(start, 16)],
            out_ref.at[tile, block],
            send_sem,
            recv_sem,
            device_id=(to_gx, to_gy, layer),
            device_id_type=MESH,
        ).start()
        return carry

    lax.fori_loop(1, 128, send, 0)
    pltpu.make_async_copy(out_ref, out_ref, recv_sem).wait()

    @pl.when(inside)
    def _():
        rest = chunks.at[pl.ds(0, 127 * 16)]
        pltpu.make_async_copy(rest, rest, send_sem).wait()

    @pl.when(jnp.logical_not(inside))
    def _():
        pltpu.make_async_copy(chunks, chunks, send_sem).wait()


def merge_kernel(
    got_ref, box_ref, speed_ref, radius_ref, steps_ref, high_ref, low_ref,
    own_ref, other_ref, radius, rows, radius_sem,
):
    gx, gy, gz = lax.axis_index("gx"), lax.axis_index("gy"), lax.axis_index("gz")
    fetch = pltpu.make_async_copy(radius_ref.at[gz], radius, radius_sem)
    fetch.start()
    first = (gx * 8 + gy) * 2
    speeds, starts = [], []
    for which in range(2):
        start = steps_ref[3]
        for axis in range(3):
            center = (box_ref[axis, first + which].astype(F32) + 0.5) / TG - 0.5
            part = steps_ref[axis] * center
            start = start + (part - jnp.round(part))
        starts.append(start - jnp.round(start))
        speeds.append(speed_ref[first + which])
    fetch.wait()
    real_side = lax.broadcasted_iota(jnp.int32, (8, 128), 1) < 64
    upper = lax.broadcasted_iota(jnp.int32, (8, 128), 0) < 4

    def group(number, carry):
        qx, ax, ay = number // 4, number // 2 % 2, number % 2
        base = (qx * 2 + ax) * 4 + ay
        row = pl.multiple_of((ax * 4 + ay * 2) * 64 + qx * 8, 8)
        for which in range(2):
            for block in range(4):
                pair = []
                for low in range(2):
                    tile = base + 2 * low
                    turns = radius[tile, block] * speeds[which] + starts[which][block][None, :]
                    wave = cosine_of_turns(turns)
                    wave_over = pltpu.roll(wave, 64, 1)
                    value = got_ref[tile, block, which * 8 : which * 8 + 8, :]
                    value_over = pltpu.roll(value, 64, 1)
                    pair.append(
                        value * jnp.where(real_side, wave, wave_over)
                        + value_over * jnp.where(real_side, -wave_over, wave)
                    )
                lanes = slice(block * 128, block * 128 + 128)
                rows[pl.ds(row + which * 32, 8), lanes] = jnp.where(
                    upper, pair[0], pltpu.roll(pair[1], 4, 0)
                )
                rows[pl.ds(row + which * 32 + 64, 8), lanes] = jnp.where(
                    upper, pltpu.roll(pair[0], 4, 0), pair[1]
                )
        return carry

    lax.fori_loop(0, 16, group, 0)
    for part in range(4):
        at = slice(part * 128, part * 128 + 128)
        taken = split(rows[at, :])
        other_ref[at, :] = dot3(taken, (high_ref[1 - gz], low_ref[1 - gz]))
        own_ref[at, :] = dot3(taken, (high_ref[gz], low_ref[gz]))


def later_kernel(own_ref, came_ref, high_ref, low_ref, out_ref, columns, done, done_sem):
    gz = lax.axis_index("gz")
    for a in range(8):
        pieces = []
        for which in range(2):
            for qx in range(4):
                at = slice(a * 64 + which * 32 + qx * 8, a * 64 + which * 32 + qx * 8 + 8)
                mine, theirs = own_ref[at, :], came_ref[at, :]
                for qy_high in range(2):
                    pieces.append(jnp.where((qx + qy_high) % 2 == gz, mine, theirs))
        flipped = jnp.concatenate(pieces, axis=0).T
        for part in range(2):
            for sigma in range(4):
                at = (part * 4 + sigma) * 32
                columns[a * 64 + part * 32 : a * 64 + part * 32 + 32, sigma * 128 : sigma * 128 + 128] = (
                    flipped[at : at + 32, :]
                )
    matrix = (high_ref[...], low_ref[...])
    first_side = lax.broadcasted_iota(jnp.int32, (56, 128), 1) < 64
    for sigma_x in range(2):
        result = dot3(matrix, split(columns[:, sigma_x * 256 : sigma_x * 256 + 256]))
        for sigma_y in range(2):
            sigma = sigma_x * 2 + sigma_y
            for tau in range(4):
                lanes = slice(sigma_y * 128, sigma_y * 128 + 128)
                down = result[tau * 56 : tau * 56 + 56, lanes]
                up = result[224 + tau * 56 : 224 + tau * 56 + 56, lanes]
                tile = sigma * 4 + tau
                done.at[tile][pl.ds(0, 54, stride=2), :] = jnp.where(
                    first_side, down, pltpu.roll(up, 64, 1)
                )[:54]
                done.at[tile][pl.ds(1, 54, stride=2), :] = jnp.where(
                    first_side, pltpu.roll(down, 64, 1), up
                )[:54]
                pltpu.make_async_copy(
                    done.at[tile], out_ref.at[:, tile * 128 : tile * 128 + 128], done_sem.at[tile]
                ).start()
    for tile in range(16):
        pltpu.make_async_copy(
            done.at[tile], out_ref.at[:, tile * 128 : tile * 128 + 128], done_sem.at[tile]
        ).wait()


VMEM = pl.BlockSpec(memory_space=pltpu.VMEM)
SMEM = pl.BlockSpec(memory_space=pltpu.SMEM)
ANY = pl.BlockSpec(memory_space=pl.ANY)


def per_device(weights, target_box, wave_speed):
    merge, later, radius, steps = tables()
    merge_high, merge_low = (jnp.asarray(part) for part in halves_of(merge))
    later_high, later_low = (jnp.asarray(part) for part in halves_of(later))
    got = pl.pallas_call(
        spread_kernel,
        out_shape=jax.ShapeDtypeStruct((32, 4, 16, 128), F32),
        in_specs=[ANY],
        out_specs=ANY,
        scratch_shapes=[
            pltpu.VMEM((2, 864, 128), F32),
            pltpu.VMEM((128, 128), F32),
            pltpu.VMEM((2048, 128), F32),
            pltpu.SemaphoreType.DMA((2,)),
            pltpu.SemaphoreType.DMA,
            pltpu.SemaphoreType.DMA,
        ],
        compiler_params=pltpu.CompilerParams(
            has_side_effects=True, vmem_limit_bytes=32 * 2**20
        ),
        name="spread",
    )(weights.reshape(864, 256))
    own, other = pl.pallas_call(
        merge_kernel,
        out_shape=[jax.ShapeDtypeStruct((512, 256), F32)] * 2,
        in_specs=[VMEM, SMEM, SMEM, ANY, VMEM, VMEM, VMEM],
        out_specs=[VMEM, VMEM],
        scratch_shapes=[
            pltpu.VMEM((32, 4, 8, 128), F32),
            pltpu.VMEM((512, 512), F32),
            pltpu.SemaphoreType.DMA,
        ],
        compiler_params=pltpu.CompilerParams(vmem_limit_bytes=32 * 2**20),
        name="merge",
    )(
        got, target_box, wave_speed, jnp.asarray(radius, F32), jnp.asarray(steps, F32),
        merge_high, merge_low,
    )
    came = lax.ppermute(other, "gz", [(0, 1), (1, 0)])
    out = pl.pallas_call(
        later_kernel,
        out_shape=jax.ShapeDtypeStruct((108, 2048), F32),
        in_specs=[VMEM] * 4,
        out_specs=ANY,
        scratch_shapes=[
            pltpu.VMEM((512, 512), F32),
            pltpu.VMEM((16, 108, 128), F32),
            pltpu.SemaphoreType.DMA((16,)),
        ],
        compiler_params=pltpu.CompilerParams(vmem_limit_bytes=32 * 2**20),
        name="later",
    )(own, came, later_high, later_low)
    return out.reshape(2, 27, 1, 2, 2048)


def solution(mesh):
    return jax.shard_map(
        per_device,
        mesh=mesh,
        in_specs=(P(None, None, "gx", "gy", "gz", None, None), P(), P()),
        out_specs=P(None, None, "gz", ("gx", "gy"), None),
        check_vma=False,
    )
```

```python
import functools
import math

import jax
import jax.numpy as jnp
import numpy as np
from jax import lax
from jax.experimental import pallas as pl
from jax.experimental.pallas import tpu as pltpu
from jax.sharding import PartitionSpec as P

TG = 16
NK = 256.0
MESH = pl.DeviceIdType.MESH
F32 = jnp.float32
BF16 = jnp.bfloat16


def chebyshev_points():
    return np.array([-math.sqrt(3.0) / 2.0, 0.0, math.sqrt(3.0) / 2.0])


def node_places():
    points = chebyshev_points()
    numbers = np.arange(27)
    return np.stack([points[numbers // 9], points[numbers // 3 % 3], points[numbers % 3]])


def lagrange_line(child_bit):
    points = chebyshev_points()
    places = child_bit - 0.5 + points / 2.0
    lagrange = np.ones((3, 3))
    for parent_node in range(3):
        for others in range(3):
            if others != parent_node:
                lagrange[parent_node, :] = (
                    lagrange[parent_node, :]
                    * (places - points[others])
                    / (points[parent_node] - points[others])
                )
    return lagrange


def child_bits(code):
    return (code // 4, code // 2 % 2, code % 2)


def child_matrix(code):
    picked = child_bits(code)
    return np.kron(
        np.kron(lagrange_line(picked[0]), lagrange_line(picked[1])), lagrange_line(picked[2])
    )


W4 = NK / 16
W5, W6 = 2 * W4, 4 * W4
H4 = 1.0 / TG
H5, H6 = H4 / 2, H4 / 4


def signs(code):
    return np.array(child_bits(code)) - 0.5


def child_step(code):
    return signs(code)[:, None] * W4 + 0.5 * W4 * node_places()


def lane_of(code, part):
    bx, by, bz = child_bits(code)
    return (bx * 2 + bz) * 128 + part * 64 + 2 * np.arange(27) + by


@functools.cache
def tables():
    places = node_places()
    turn = np.exp(2j * math.pi * H5 * W5 / 4.0 * (places.T @ places))
    parity = {}
    for sigma in range(8):
        row = [np.exp(2j * math.pi * (signs(sigma) * H4 / 2) @ (signs(a) * W5)) for a in range(8)]
        parity[sigma] = np.array(row)
    along = parity[0] / parity[0][0]
    merge = np.zeros((2, 512, 4, 2, 32))
    for sigma in range(8):
        assert np.allclose(parity[sigma], parity[sigma][0] * along)
        for code in range(8):
            shift = np.exp(2j * math.pi * (signs(sigma) * H4 / 2) @ child_step(code))
            both = (turn @ child_matrix(code)) * shift[None, :] * parity[sigma][0] * -1.0
            half = merge[sigma % 2]
            real, imag = lane_of(code, 0), lane_of(code, 1)
            half[real, sigma // 2, 0, :27] = both.real.T
            half[real, sigma // 2, 1, :27] = both.imag.T
            half[imag, sigma // 2, 0, :27] = -both.imag.T
            half[imag, sigma // 2, 1, :27] = both.real.T
    merge = merge.reshape(2, 512, 256)
    later = np.zeros((2, 4, 56, 8, 2, 32))
    for tau in range(8):
        spot = (signs(tau) * H5 / 2)[:, None] + H6 / 2 * places
        for a in range(8):
            shift = np.exp(2j * math.pi * (signs(a) * W5) @ spot) * along[a]
            both = child_matrix(tau).T * shift[:, None]
            block = later[tau % 2, tau // 2]
            block[:27, a, 0, :27] = both.real
            block[:27, a, 1, :27] = -both.imag
            block[27:54, a, 0, :27] = both.imag
            block[27:54, a, 1, :27] = both.real
    later = later.reshape(448, 512)
    radius = np.zeros((2, 4, 2, 2, 2, 4, 2, 4, 128))
    steps = np.zeros((4, 4, 128))
    for code in range(8):
        bx, by, bz = child_bits(code)
        offset = child_step(code)
        for part in range(2):
            lanes = lane_of(code, part) % 128
            steps[:3, bx * 2 + bz, lanes] = offset
            for gz, qx, ax, qylo, ay, az, qz in np.ndindex(2, 4, 2, 2, 2, 2, 4):
                q = np.array([qx, 2 * ((gz + qx) % 2) + qylo, qz])
                center = -NK / 2 + (2 * q + np.array([ax, ay, az]) + 0.5) * W5
                anchor = -NK / 2 + (q + 0.5) * W6
                node = center[:, None] + offset
                radius[gz, qx, ax, qylo, ay, bx * 2 + bz, az, qz, lanes] = np.sqrt(
                    (node**2).sum(0)
                ) - np.sqrt((anchor**2).sum())
    steps[3, :, 64:] = -0.25
    return merge, later, radius.reshape(2, 32, 4, 8, 128), steps


@functools.cache
def cosine_terms():
    nodes = np.cos((np.arange(400) + 0.5) * math.pi / 400) * 0.125 + 0.125
    fitted = np.polynomial.Polynomial.fit(nodes, np.cos(2 * math.pi * np.sqrt(nodes)), 7)
    return [float(c) for c in fitted.convert().coef]


def cosine_of_turns(turns):
    turns = turns - jnp.round(turns)
    square = turns * turns
    terms = cosine_terms()
    total = terms[-1]
    for term in terms[-2::-1]:
        total = total * square + term
    return total


def halves_of(matrix):
    wide = np.asarray(matrix, np.float32)
    high = wide.astype(jnp.bfloat16)
    low = (wide - high.astype(np.float32)).astype(jnp.bfloat16)
    return high, low


def split(x):
    high = x.astype(BF16)
    return high, (x - high.astype(F32)).astype(BF16)


def dot3(a, b):
    out = jnp.dot(a[0], b[0], preferred_element_type=F32)
    out += jnp.dot(a[0], b[1], preferred_element_type=F32)
    return out + jnp.dot(a[1], b[0], preferred_element_type=F32)


def window_kernel(
    w_ref, box_ref, speed_ref, radius_ref, steps_ref, merge_ref, later_ref, out_ref,
    taken, turned, chunks, got, radius, steps, merge, later, wave, rows,
    own, other, came, columns, done,
    take_sem, table_sem, send_sem, recv_sem, swap_send, swap_recv, done_sem,
):
    gx, gy, gz = lax.axis_index("gx"), lax.axis_index("gy"), lax.axis_index("gz")
    z, y, x, core = gx // 4, gx % 4, gy // 2, gy % 2
    tile = ((gx // 2) * 2 + gy // 2 % 2) * 2 + gy % 2
    block = gx % 2 * 2 + gz
    layer = (z + gy // 4) % 2
    inside = layer == gz

    barrier = pltpu.get_barrier_semaphore()

    def tell(to_z, to_y, to_x_low, to_core, to_gz):
        to_x = 2 * lax.rem(to_z + gz, 2) + to_x_low
        pl.semaphore_signal(
            barrier,
            inc=1,
            device_id=(to_z * 4 + to_y, to_x * 2 + to_core, to_gz),
            device_id_type=MESH,
        )

    @pl.when(jnp.logical_not(inside))
    def _():
        tell(z, y, lax.rem(x, 2), core, gz)
        pl.semaphore_signal(barrier, inc=1, device_id=(gx, gy, 1 - gz), device_id_type=MESH)

    def tell_all(step, carry):
        to_z = lax.rem(z + step, 4)
        to_x_low = lax.rem(x + step // 4, 2)
        to_core = lax.rem(core + step // 8, 2)
        for more in range(4):
            for flip in range(2):
                tell(to_z, lax.rem(y + more, 4), to_x_low, to_core, lax.rem(gz + flip, 2))
        return carry

    tell(z, y, lax.rem(x, 2), core, 1 - gz)
    for more in range(1, 4):
        for flip in range(2):
            tell(z, lax.rem(y + more, 4), lax.rem(x, 2), core, lax.rem(gz + flip, 2))
    lax.fori_loop(1, 16, tell_all, 0)

    takes = [
        pltpu.make_async_copy(
            w_ref.at[:, half * 128 : half * 128 + 128], taken.at[half], take_sem.at[half]
        )
        for half in range(2)
    ]
    fetches = [
        pltpu.make_async_copy(source, target, table_sem.at[number])
        for number, (source, target) in enumerate(
            [
                (radius_ref.at[gz], radius),
                (steps_ref, steps),
                (merge_ref, merge),
                (later_ref, later),
            ]
        )
    ]
    for copy in takes + fetches:
        copy.start()
    turned[...] = jnp.zeros_like(turned)
    for half in range(2):
        takes[half].wait()
        for depth in range(8):
            turned[0:54, :] = taken.at[half][pl.ds(depth, 54, stride=8), :]
            turned[64:118, :] = taken.at[half][pl.ds(432 + depth, 54, stride=8), :]
            row = half * 1024 + depth % 2 * 4 + depth // 2
            chunks[pl.ds(row, 128, stride=8), :] = turned[...].T

    pl.semaphore_wait(barrier, 128)

    def chunk(to_gx, to_gy, which):
        return chunks.at[pl.ds(pl.multiple_of((to_gx * 8 + to_gy) * 16 + which * 8, 8), 8)]

    def send(to_z, to_y, to_x, to_core, which):
        to_gx, to_gy = to_z * 4 + to_y, to_x * 2 + to_core
        pltpu.make_async_remote_copy(
            chunk(to_gx, to_gy, which),
            got.at[which, tile, block],
            send_sem,
            recv_sem.at[which],
            device_id=(to_gx, to_gy, layer),
            device_id_type=MESH,
        ).start()

    for which in range(2):

        @pl.when(inside)
        def _():
            pltpu.make_async_copy(
                chunk(gx, gy, which), got.at[which, tile, block], recv_sem.at[which]
            ).start()

        @pl.when(jnp.logical_not(inside))
        def _():
            send(z, y, x, core, which)

        for more in range(1, 4):
            send(lax.rem(z + more, 4), y, x, core, which)

        def send_all(step, carry):
            to_x = lax.rem(x + step, 4)
            to_y = lax.rem(y + step // 4, 4)
            to_core = lax.rem(core + step // 16, 2)
            for more in range(4):
                send(lax.rem(z + more, 4), to_y, to_x, to_core, which)
            return carry

        lax.fori_loop(1, 32, send_all, 0)

    fetches[0].wait()
    fetches[1].wait()
    first = (gx * 8 + gy) * 2
    real_side = lax.broadcasted_iota(jnp.int32, (8, 128), 1) < 64
    upper = lax.broadcasted_iota(jnp.int32, (8, 128), 0) < 4
    for which in range(2):
        start = steps[3]
        for axis in range(3):
            center = (box_ref[axis, first + which].astype(F32) + 0.5) / TG - 0.5
            part = steps[axis] * center
            start = start + (part - jnp.round(part))
        start = start - jnp.round(start)
        speed = speed_ref[first + which]

        def make(number, carry):
            for side in range(4):
                turns = radius[number, side] * speed + start[side][None, :]
                value = cosine_of_turns(turns)
                over = pltpu.roll(value, 64, 1)
                wave[0, which, number, side] = jnp.where(real_side, value, over)
                wave[1, which, number, side] = jnp.where(real_side, -over, value)
            return carry

        lax.fori_loop(0, 32, make, 0)
    fetches[2].wait()
    fetches[3].wait()

    swaps = []
    for which in range(2):
        pltpu.make_async_copy(got.at[which], got.at[which], recv_sem.at[which]).wait()

        def group(number, carry):
            qx, ax, ay = number // 4, number // 2 % 2, number % 2
            base = (qx * 2 + ax) * 4 + ay
            row = pl.multiple_of((ax * 4 + ay * 2) * 32 + qx * 8, 8)
            for side in range(4):
                pair = []
                for low in range(2):
                    at = base + 2 * low
                    value = got[which, at, side]
                    pair.append(
                        value * wave[0, which, at, side]
                        + pltpu.roll(value, 64, 1) * wave[1, which, at, side]
                    )
                lanes = slice(side * 128, side * 128 + 128)
                rows[pl.ds(row, 8), lanes] = jnp.where(
                    upper, pair[0], pltpu.roll(pair[1], 4, 0)
                )
                rows[pl.ds(row + 32, 8), lanes] = jnp.where(
                    upper, pltpu.roll(pair[0], 4, 0), pair[1]
                )
            return carry

        lax.fori_loop(0, 16, group, 0)
        for part in range(2):
            at = pl.ds(part * 128, 128)
            taken_rows = split(rows[at, :])
            other[which, at] = dot3(taken_rows, (merge[0, 1 - gz], merge[1, 1 - gz]))
            swap = pltpu.make_async_remote_copy(
                other.at[which, at],
                came.at[which, at],
                swap_send.at[which, part],
                swap_recv.at[which, part],
                device_id=(gx, gy, 1 - gz),
                device_id_type=MESH,
            )
            swap.start()
            swaps.append(swap)
            own[which, at] = dot3(taken_rows, (merge[0, gz], merge[1, gz]))

    matrix = (later[0], later[1])
    lane_low = lax.broadcasted_iota(jnp.int32, (64, 128), 1) < 64
    first_side = lax.broadcasted_iota(jnp.int32, (56, 128), 1) < 64

    def leave(number):
        return pltpu.make_async_copy(
            done.at[number], out_ref.at[:, number * 128 : number * 128 + 128], done_sem.at[number]
        )

    for which in range(2):
        for couple in range(4):
            if couple % 2 == 0:
                swaps[which * 2 + couple // 2].wait()
            stacked = []
            for a in (2 * couple, 2 * couple + 1):
                pieces = []
                for qx in range(4):
                    at = slice(a * 32 + qx * 8, a * 32 + qx * 8 + 8)
                    mine, theirs = own[which, at], came[which, at]
                    for qy_high in range(2):
                        pieces.append(jnp.where((qx + qy_high) % 2 == gz, mine, theirs))
                stacked.append(jnp.concatenate(pieces, axis=0))
            for sigma_x in range(2):
                lanes = slice(sigma_x * 128, sigma_x * 128 + 128)
                even, odd = stacked[0][:, lanes], stacked[1][:, lanes]
                both = jnp.concatenate(
                    [
                        jnp.where(lane_low, even, pltpu.roll(odd, 64, 1)),
                        jnp.where(lane_low, pltpu.roll(even, 64, 1), odd),
                    ],
                    axis=0,
                )
                columns[couple * 128 : couple * 128 + 128, lanes] = both.T
        result = dot3(matrix, split(columns[...]))
        for sigma_x in range(2):
            lanes = slice(sigma_x * 128, sigma_x * 128 + 128)
            for tau in range(4):
                down = result[tau * 56 : tau * 56 + 56, lanes]
                up = result[224 + tau * 56 : 224 + tau * 56 + 56, lanes]
                number = sigma_x * 8 + tau
                done.at[number][pl.ds(which, 54, stride=2), :] = jnp.where(
                    first_side, down, pltpu.roll(up, 64, 1)
                )[:54]
                done.at[number + 4][pl.ds(which, 54, stride=2), :] = jnp.where(
                    first_side, pltpu.roll(down, 64, 1), up
                )[:54]
                if which == 1:
                    leave(number).start()
                    leave(number + 4).start()
    for number in range(16):
        leave(number).wait()

    @pl.when(inside)
    def _():
        rest = chunks.at[pl.ds(0, 254 * 8)]
        pltpu.make_async_copy(rest, rest, send_sem).wait()

    @pl.when(jnp.logical_not(inside))
    def _():
        pltpu.make_async_copy(chunks, chunks, send_sem).wait()


SMEM = pl.BlockSpec(memory_space=pltpu.SMEM)
ANY = pl.BlockSpec(memory_space=pl.ANY)


def per_device(weights, target_box, wave_speed):
    merge, later, radius, steps = tables()
    out = pl.pallas_call(
        window_kernel,
        out_shape=jax.ShapeDtypeStruct((108, 2048), F32),
        in_specs=[ANY, SMEM, SMEM, ANY, ANY, ANY, ANY],
        out_specs=ANY,
        scratch_shapes=[
            pltpu.VMEM((2, 864, 128), F32),
            pltpu.VMEM((128, 128), F32),
            pltpu.VMEM((2048, 128), F32),
            pltpu.VMEM((2, 32, 4, 8, 128), F32),
            pltpu.VMEM((32, 4, 8, 128), F32),
            pltpu.VMEM((4, 4, 128), F32),
            pltpu.VMEM((2, 2, 512, 256), BF16),
            pltpu.VMEM((2, 448, 512), BF16),
            pltpu.VMEM((2, 2, 32, 4, 8, 128), F32),
            pltpu.VMEM((256, 512), F32),
            pltpu.VMEM((2, 256, 256), F32),
            pltpu.VMEM((2, 256, 256), F32),
            pltpu.VMEM((2, 256, 256), F32),
            pltpu.VMEM((512, 256), F32),
            pltpu.VMEM((16, 108, 128), F32),
            pltpu.SemaphoreType.DMA((2,)),
            pltpu.SemaphoreType.DMA((4,)),
            pltpu.SemaphoreType.DMA,
            pltpu.SemaphoreType.DMA((2,)),
            pltpu.SemaphoreType.DMA((2, 2)),
            pltpu.SemaphoreType.DMA((2, 2)),
            pltpu.SemaphoreType.DMA((16,)),
        ],
        compiler_params=pltpu.CompilerParams(
            collective_id=0, has_side_effects=True, vmem_limit_bytes=58 * 2**20
        ),
        name="window",
    )(
        weights.reshape(864, 256),
        target_box,
        wave_speed,
        jnp.asarray(radius, F32),
        jnp.asarray(steps, F32),
        jnp.asarray(np.stack(halves_of(merge))),
        jnp.asarray(np.stack(halves_of(later))),
    )
    return out.reshape(2, 27, 1, 2, 2048)


def solution(mesh):
    return jax.shard_map(
        per_device,
        mesh=mesh,
        in_specs=(P(None, None, "gx", "gy", "gz", None, None), P(), P()),
        out_specs=P(None, None, "gz", ("gx", "gy"), None),
        check_vma=False,
    )
```

```python
import functools
import math

import jax
import jax.numpy as jnp
import numpy as np
from jax import lax
from jax.experimental import pallas as pl
from jax.experimental.pallas import tpu as pltpu
from jax.sharding import PartitionSpec as P

TG = 16
NK = 256.0
MESH = pl.DeviceIdType.MESH
F32 = jnp.float32
BF16 = jnp.bfloat16


def chebyshev_points():
    return np.array([-math.sqrt(3.0) / 2.0, 0.0, math.sqrt(3.0) / 2.0])


def node_places():
    points = chebyshev_points()
    numbers = np.arange(27)
    return np.stack([points[numbers // 9], points[numbers // 3 % 3], points[numbers % 3]])


def lagrange_line(child_bit):
    points = chebyshev_points()
    places = child_bit - 0.5 + points / 2.0
    lagrange = np.ones((3, 3))
    for parent_node in range(3):
        for others in range(3):
            if others != parent_node:
                lagrange[parent_node, :] = (
                    lagrange[parent_node, :]
                    * (places - points[others])
                    / (points[parent_node] - points[others])
                )
    return lagrange


def child_bits(code):
    return (code // 4, code // 2 % 2, code % 2)


def child_matrix(code):
    picked = child_bits(code)
    return np.kron(
        np.kron(lagrange_line(picked[0]), lagrange_line(picked[1])), lagrange_line(picked[2])
    )


W4 = NK / 16
W5, W6 = 2 * W4, 4 * W4
H4 = 1.0 / TG
H5, H6 = H4 / 2, H4 / 4


def signs(code):
    return np.array(child_bits(code)) - 0.5


def child_step(code):
    return signs(code)[:, None] * W4 + 0.5 * W4 * node_places()


def lane_of(code, part):
    bx, by, bz = child_bits(code)
    return (bx * 2 + bz) * 128 + part * 64 + 2 * np.arange(27) + by


@functools.cache
def tables():
    places = node_places()
    turn = np.exp(2j * math.pi * H5 * W5 / 4.0 * (places.T @ places))
    parity = {}
    for sigma in range(8):
        row = [np.exp(2j * math.pi * (signs(sigma) * H4 / 2) @ (signs(a) * W5)) for a in range(8)]
        parity[sigma] = np.array(row)
    along = parity[0] / parity[0][0]
    merge = np.zeros((2, 512, 4, 2, 32))
    for sigma in range(8):
        assert np.allclose(parity[sigma], parity[sigma][0] * along)
        for code in range(8):
            shift = np.exp(2j * math.pi * (signs(sigma) * H4 / 2) @ child_step(code))
            both = (turn @ child_matrix(code)) * shift[None, :] * parity[sigma][0] * -1.0
            half = merge[sigma % 2]
            real, imag = lane_of(code, 0), lane_of(code, 1)
            half[real, sigma // 2, 0, :27] = both.real.T
            half[real, sigma // 2, 1, :27] = both.imag.T
            half[imag, sigma // 2, 0, :27] = -both.imag.T
            half[imag, sigma // 2, 1, :27] = both.real.T
    merge = merge.reshape(2, 512, 256)
    later = np.zeros((2, 4, 56, 8, 2, 32))
    for tau in range(8):
        spot = (signs(tau) * H5 / 2)[:, None] + H6 / 2 * places
        for a in range(8):
            shift = np.exp(2j * math.pi * (signs(a) * W5) @ spot) * along[a]
            both = child_matrix(tau).T * shift[:, None]
            block = later[tau % 2, tau // 2]
            block[:27, a, 0, :27] = both.real
            block[:27, a, 1, :27] = -both.imag
            block[27:54, a, 0, :27] = both.imag
            block[27:54, a, 1, :27] = both.real
    later = later.reshape(448, 512)
    radius = np.zeros((4, 2, 2, 2, 2, 4, 2, 4, 128))
    steps = np.zeros((4, 4, 128))
    for code in range(8):
        bx, by, bz = child_bits(code)
        offset = child_step(code)
        for part in range(2):
            lanes = lane_of(code, part) % 128
            steps[:3, bx * 2 + bz, lanes] = offset
            for qx, qyhi, ax, qylo, ay, az, qz in np.ndindex(4, 2, 2, 2, 2, 2, 4):
                q = np.array([qx, 2 * qyhi + qylo, qz])
                center = -NK / 2 + (2 * q + np.array([ax, ay, az]) + 0.5) * W5
                anchor = -NK / 2 + (q + 0.5) * W6
                node = center[:, None] + offset
                radius[qx, qyhi, ax, qylo, ay, bx * 2 + bz, az, qz, lanes] = np.sqrt(
                    (node**2).sum(0)
                ) - np.sqrt((anchor**2).sum())
    steps[3, :, 64:] = -0.25
    return merge, later, radius.reshape(4, 2, 2, 4, 4, 8, 128), steps


@functools.cache
def cosine_terms():
    nodes = np.cos((np.arange(400) + 0.5) * math.pi / 400) * 0.125 + 0.125
    fitted = np.polynomial.Polynomial.fit(nodes, np.cos(2 * math.pi * np.sqrt(nodes)), 7)
    return [float(c) for c in fitted.convert().coef]


def cosine_of_turns(turns):
    turns = turns - jnp.round(turns)
    square = turns * turns
    terms = cosine_terms()
    total = terms[-1]
    for term in terms[-2::-1]:
        total = total * square + term
    return total


def halves_of(matrix):
    wide = np.asarray(matrix, np.float32)
    high = wide.astype(jnp.bfloat16)
    low = (wide - high.astype(np.float32)).astype(jnp.bfloat16)
    return high, low


def split(x):
    high = x.astype(BF16)
    return high, (x - high.astype(F32)).astype(BF16)


def window_kernel(
    w_ref, box_ref, speed_ref, radius_ref, steps_ref, merge_ref, later_ref, out_ref,
    taken, turned, chunks, got, radius, steps, merge, later, wave, rows,
    mid, other, columns, total, done,
    take_sem, table_sem, send_sem, recv_sem, swap_send, swap_recv, done_sem,
):
    gx, gy, gz = lax.axis_index("gx"), lax.axis_index("gy"), lax.axis_index("gz")
    z, y, x, core = gx // 4, gx % 4, gy // 2, gy % 2
    ax, high = gx // 2 % 2, gy // 4
    place = gy // 2 % 2 * 2 + core
    block = gx % 2 * 2 + gz
    even = lax.rem(high + z, 2)
    inside = even == gz
    beside = lax.rem(z + 3 - 2 * gz, 4)
    side_high = lax.rem(gz + z, 2)
    groups = [(z, side_high), (lax.rem(z + 2, 4), side_high), (beside, 0), (beside, 1)]

    barrier = pltpu.get_barrier_semaphore()

    def tell(to_z, to_y, to_x, to_core, to_gz):
        pl.semaphore_signal(
            barrier,
            inc=1,
            device_id=(to_z * 4 + to_y, to_x * 2 + to_core, to_gz),
            device_id_type=MESH,
        )

    x_low = lax.rem(x, 2)

    @pl.when(jnp.logical_not(inside))
    def _():
        tell(z, y, 2 * side_high + x_low, core, gz)
        tell(z, y, x, core, 1 - gz)

    tell(z, y, 2 * side_high + x_low, core, 1 - gz)
    for number, (to_z, to_high) in enumerate(groups):
        for more in range(4):
            for flip in range(2):
                if number + more > 0:
                    tell(
                        to_z, lax.rem(y + more, 4), 2 * to_high + x_low, core,
                        lax.rem(gz + flip, 2),
                    )

    def tell_all(step, carry):
        to_low = lax.rem(x + step, 2)
        to_core = lax.rem(core + step // 2, 2)
        for to_z, to_high in groups:
            for more in range(4):
                for flip in range(2):
                    tell(
                        to_z, lax.rem(y + more, 4), 2 * to_high + to_low, to_core,
                        lax.rem(gz + flip, 2),
                    )
        return carry

    lax.fori_loop(1, 4, tell_all, 0)

    takes = [
        pltpu.make_async_copy(
            w_ref.at[:, half * 128 : half * 128 + 128], taken.at[half], take_sem.at[half]
        )
        for half in range(2)
    ]
    sources = [(steps_ref, steps), (merge_ref, merge), (later_ref, later)]
    sources += [(radius_ref.at[qx, qy], radius.at[k]) for k, (qx, qy) in enumerate(groups)]
    fetches = [
        pltpu.make_async_copy(source, target, table_sem.at[number])
        for number, (source, target) in enumerate(sources)
    ]
    for copy in takes + fetches:
        copy.start()
    turned[...] = jnp.zeros_like(turned)
    for half in range(2):
        takes[half].wait()
        for row in range(7):
            depth = row % 4 * 2 + row // 4
            turned[0:54, :] = taken.at[half][pl.ds(depth, 54, stride=8), :]
            turned[64:118, :] = taken.at[half][pl.ds(432 + depth, 54, stride=8), :]
            if row < 6:
                last = 72 * row + 7
                turned[54:63, :] = taken.at[half][pl.ds(432 + last, 9, stride=8), :]
                turned[118:127, :] = taken.at[half][pl.ds(last, 9, stride=8), :]
            chunks[pl.ds(half * 1024 + row, 128, stride=8), :] = turned[...].T

    first = (gx * 8 + gy) * 2
    real_side = lax.broadcasted_iota(jnp.int32, (8, 128), 1) < 64
    upper = lax.broadcasted_iota(jnp.int32, (8, 128), 0) < 4

    def make_wave(which):
        start = steps[3]
        for axis in range(3):
            center = (box_ref[axis, first + which].astype(F32) + 0.5) / TG - 0.5
            part = steps[axis] * center
            start = start + (part - jnp.round(part))
        start = (start - jnp.round(start))[None, :, None, :]
        speed = speed_ref[first + which]

        def make(number, carry):
            value = cosine_of_turns(radius[number // 2, number % 2] * speed + start)
            over = pltpu.roll(value, 64, 3)
            wave[0, which, number % 2, number // 2] = jnp.where(real_side, value, over)
            wave[1, which, number % 2, number // 2] = jnp.where(real_side, -over, value)
            return carry

        lax.fori_loop(0, 8, make, 0)

    fetches[0].wait()
    for fetch in fetches[3:]:
        fetch.wait()
    make_wave(0)
    pl.semaphore_wait(barrier, 128)

    def chunk(to_gx, to_gy, which):
        return chunks.at[pl.ds(pl.multiple_of((to_gx * 8 + to_gy) * 16 + which * 8, 8), 7)]

    def send(more, to_y, to_x, to_core, which, turn):
        to_gx, to_gy = lax.rem(z + more, 4) * 4 + to_y, to_x * 2 + to_core
        slot = (0, 2 + high, 1, 2 + high)[more]
        layer = (even, 0, even, 1)[more]
        pltpu.make_async_remote_copy(
            chunk(to_gx, to_gy, which),
            got.at[which, ax, slot * 4 + place, block, 0:7],
            send_sem,
            recv_sem.at[which, turn],
            device_id=(to_gx, to_gy, layer),
            device_id_type=MESH,
        ).start()

    for which in range(2):
        for turn in range(2):
            to_core = lax.rem(ax + turn, 2)
            itself = jnp.logical_and(inside, to_core == core)

            @pl.when(itself)
            def _():
                pltpu.make_async_copy(
                    chunk(gx, gy, which),
                    got.at[which, ax, place, block, 0:7],
                    recv_sem.at[which, turn],
                ).start()

            @pl.when(jnp.logical_not(itself))
            def _():
                send(0, y, x, to_core, which, turn)

            for more in range(1, 4):
                send(more, y, x, to_core, which, turn)

            def send_all(step, carry):
                to_x = lax.rem(x + step, 4)
                to_y = lax.rem(y + step // 4, 4)
                for more in range(4):
                    send(more, to_y, to_x, to_core, which, turn)
                return carry

            lax.fori_loop(1, 16, send_all, 0)

    make_wave(1)
    fetches[1].wait()
    fetches[2].wait()
    sublane = lax.broadcasted_iota(jnp.int32, (8, 128), 0)
    entry = lax.broadcasted_iota(jnp.int32, (8, 128), 1) % 64
    packed = (sublane < 6) & (entry >= 9 * sublane) & (entry < 9 * sublane + 9)
    lane_low = lax.broadcasted_iota(jnp.int32, (64, 128), 1) < 64
    first_side = lax.broadcasted_iota(jnp.int32, (56, 128), 1) < 64

    def swap(which, turn):
        part = lax.rem(turn + core, 2)
        return pltpu.make_async_remote_copy(
            other.at[which, part],
            mid.at[gz, which, part],
            swap_send.at[which, turn],
            swap_recv.at[which, turn],
            device_id=(gx, gy, 1 - gz),
            device_id_type=MESH,
        )

    def merge_part(which, turn):
        part = lax.rem(turn + core, 2)
        landed = got.at[which, part, :, :, 0:7]
        pltpu.make_async_copy(landed, landed, recv_sem.at[which, turn]).wait()

        def group(slot, carry):
            for ay in range(2):
                row = pl.multiple_of(ay * 64 + slot * 8, 8)
                for side in range(4):
                    pair = []
                    for low in range(2):
                        at = 2 * low + ay
                        value = got[which, part, slot * 4 + at, side]
                        moved = pltpu.roll(value, 10, 1, stride=9, stride_axis=0)
                        moved = jnp.where(packed, moved, 0.0)
                        last = jnp.sum(moved, axis=0, keepdims=True)
                        value = jnp.where(sublane == 7, last, value)
                        pair.append(
                            value * wave[0, which, part, slot, at, side]
                            + pltpu.roll(value, 64, 1) * wave[1, which, part, slot, at, side]
                        )
                    lanes = slice(side * 128, side * 128 + 128)
                    rows[pl.ds(row, 8), lanes] = jnp.where(
                        upper, pair[0], pltpu.roll(pair[1], 4, 0)
                    )
                    rows[pl.ds(row + 32, 8), lanes] = jnp.where(
                        upper, pltpu.roll(pair[0], 4, 0), pair[1]
                    )
            return carry

        lax.fori_loop(0, 4, group, 0)
        high_rows, low_rows = split(rows[...])
        both_rows = jnp.concatenate([high_rows, low_rows], axis=0)

        def product(side):
            out = jnp.dot(both_rows, merge[0, side], preferred_element_type=F32)
            rest = jnp.dot(high_rows, merge[1, side], preferred_element_type=F32)
            return out[:128] + out[128:] + rest

        other[which, part] = product(1 - gz)
        swap(which, turn).start()
        mid[gz, which, part] = product(gz)

    def leave(number):
        return pltpu.make_async_copy(
            done.at[number].reshape(54, 2, 128),
            out_ref.at[:, :, number * 128 : number * 128 + 128],
            done_sem.at[number],
        )

    def later_part(which, turn):
        part = lax.rem(turn + core, 2)
        swap(which, turn).wait()
        for couple in range(2):
            stacked = []
            for a in (2 * couple, 2 * couple + 1):
                pieces = []
                for qx in range(4):
                    away = lax.rem(qx + 4 - z, 4)
                    odd = lax.rem(away, 2)
                    for qy in range(2):
                        owner = (1 - odd) * ((qx + qy) % 2) + odd * (1 - away // 2)
                        slot = (1 - odd) * (away // 2) + odd * (2 + qy)
                        at = pl.multiple_of(a * 32 + slot * 8, 8)
                        pieces.append(mid[owner, which, part, pl.ds(at, 8), :])
                stacked.append(jnp.concatenate(pieces, axis=0))
            for sigma_x in range(2):
                lanes = slice(sigma_x * 128, sigma_x * 128 + 128)
                even, odd = stacked[0][:, lanes], stacked[1][:, lanes]
                both = jnp.concatenate(
                    [
                        jnp.where(lane_low, even, pltpu.roll(odd, 64, 1)),
                        jnp.where(lane_low, pltpu.roll(even, 64, 1), odd),
                    ],
                    axis=0,
                )
                columns[couple * 128 : couple * 128 + 128, lanes] = both.T
        high_part, low_part = split(columns[...])
        result = jnp.dot(later[part], high_part, preferred_element_type=F32)
        result = result[:448] + result[448:]
        result += jnp.dot(later[part, :448], low_part, preferred_element_type=F32)
        if turn == 0:
            total[...] = result
            return
        result = result + total[...]
        for sigma_x in range(2):
            lanes = slice(sigma_x * 128, sigma_x * 128 + 128)
            for tau in range(4):
                down = result[tau * 56 : tau * 56 + 56, lanes]
                up = result[224 + tau * 56 : 224 + tau * 56 + 56, lanes]
                number = sigma_x * 8 + tau
                done.at[number][pl.ds(which, 54, stride=2), :] = jnp.where(
                    first_side, down, pltpu.roll(up, 64, 1)
                )[:54]
                done.at[number + 4][pl.ds(which, 54, stride=2), :] = jnp.where(
                    first_side, pltpu.roll(down, 64, 1), up
                )[:54]
                if which == 1:
                    leave(number).start()
                    leave(number + 4).start()

    merge_part(0, 0)
    merge_part(0, 1)
    later_part(0, 0)
    merge_part(1, 0)
    later_part(0, 1)
    merge_part(1, 1)
    later_part(1, 0)
    later_part(1, 1)
    for number in range(16):
        leave(number).wait()

    @pl.when(inside)
    def _():
        rest = chunks.at[pl.ds(0, 254 * 7)]
        pltpu.make_async_copy(rest, rest, send_sem).wait()

    @pl.when(jnp.logical_not(inside))
    def _():
        rest = chunks.at[pl.ds(0, 256 * 7)]
        pltpu.make_async_copy(rest, rest, send_sem).wait()


SMEM = pl.BlockSpec(memory_space=pltpu.SMEM)
ANY = pl.BlockSpec(memory_space=pl.ANY)


def per_device(weights, target_box, wave_speed):
    merge, later, radius, steps = tables()
    out = pl.pallas_call(
        window_kernel,
        out_shape=jax.ShapeDtypeStruct((54, 2, 2048), F32),
        in_specs=[ANY, SMEM, SMEM, ANY, ANY, ANY, ANY],
        out_specs=ANY,
        scratch_shapes=[
            pltpu.VMEM((2, 864, 128), F32),
            pltpu.VMEM((128, 128), F32),
            pltpu.VMEM((2048, 128), F32),
            pltpu.VMEM((2, 2, 16, 4, 8, 128), F32),
            pltpu.VMEM((4, 2, 4, 4, 8, 128), F32),
            pltpu.VMEM((4, 4, 128), F32),
            pltpu.VMEM((2, 2, 512, 256), BF16),
            pltpu.VMEM((2, 896, 256), BF16),
            pltpu.VMEM((2, 2, 2, 4, 4, 4, 8, 128), F32),
            pltpu.VMEM((128, 512), F32),
            pltpu.VMEM((2, 2, 2, 128, 256), F32),
            pltpu.VMEM((2, 2, 128, 256), F32),
            pltpu.VMEM((256, 256), F32),
            pltpu.VMEM((448, 256), F32),
            pltpu.VMEM((16, 108, 128), F32),
            pltpu.SemaphoreType.DMA((2,)),
            pltpu.SemaphoreType.DMA((7,)),
            pltpu.SemaphoreType.DMA,
            pltpu.SemaphoreType.DMA((2, 2)),
            pltpu.SemaphoreType.DMA((2, 2)),
            pltpu.SemaphoreType.DMA((2, 2)),
            pltpu.SemaphoreType.DMA((16,)),
        ],
        compiler_params=pltpu.CompilerParams(
            collective_id=0, has_side_effects=True, vmem_limit_bytes=58 * 2**20
        ),
        name="window",
    )(
        weights.reshape(864, 256),
        target_box,
        wave_speed,
        jnp.asarray(radius, F32),
        jnp.asarray(steps, F32),
        jnp.asarray(np.stack(halves_of(merge))),
        jnp.asarray(np.concatenate(halves_of(later.reshape(448, 2, 256).swapaxes(0, 1)), axis=1)),
    )
    return out.reshape(2, 27, 1, 2, 2048)


def solution(mesh):
    return jax.shard_map(
        per_device,
        mesh=mesh,
        in_specs=(P(None, None, "gx", "gy", "gz", None, None), P(), P()),
        out_specs=P(None, None, "gz", ("gx", "gy"), None),
        check_vma=False,
    )
```

```python
import functools
import math

import jax
import jax.numpy as jnp
import numpy as np
from jax import lax
from jax.experimental import pallas as pl
from jax.experimental.pallas import tpu as pltpu
from jax.sharding import PartitionSpec as P

TG = 16
NK = 256.0
MESH = pl.DeviceIdType.MESH
F32 = jnp.float32
BF16 = jnp.bfloat16


def chebyshev_points():
    return np.array([-math.sqrt(3.0) / 2.0, 0.0, math.sqrt(3.0) / 2.0])


def node_places():
    points = chebyshev_points()
    numbers = np.arange(27)
    return np.stack([points[numbers // 9], points[numbers // 3 % 3], points[numbers % 3]])


def lagrange_line(child_bit):
    points = chebyshev_points()
    places = child_bit - 0.5 + points / 2.0
    lagrange = np.ones((3, 3))
    for parent_node in range(3):
        for others in range(3):
            if others != parent_node:
                lagrange[parent_node, :] = (
                    lagrange[parent_node, :]
                    * (places - points[others])
                    / (points[parent_node] - points[others])
                )
    return lagrange


def child_bits(code):
    return (code // 4, code // 2 % 2, code % 2)


def child_matrix(code):
    picked = child_bits(code)
    return np.kron(
        np.kron(lagrange_line(picked[0]), lagrange_line(picked[1])), lagrange_line(picked[2])
    )


W4 = NK / 16
W5, W6 = 2 * W4, 4 * W4
H4 = 1.0 / TG
H5, H6 = H4 / 2, H4 / 4


def signs(code):
    return np.array(child_bits(code)) - 0.5


def child_step(code):
    return signs(code)[:, None] * W4 + 0.5 * W4 * node_places()


def lane_of(code, part):
    bx, by, bz = child_bits(code)
    return (bx * 2 + bz) * 128 + part * 64 + 2 * np.arange(27) + by


@functools.cache
def tables():
    places = node_places()
    turn = np.exp(2j * math.pi * H5 * W5 / 4.0 * (places.T @ places))
    parity = {}
    for sigma in range(8):
        row = [np.exp(2j * math.pi * (signs(sigma) * H4 / 2) @ (signs(a) * W5)) for a in range(8)]
        parity[sigma] = np.array(row)
    along = parity[0] / parity[0][0]
    merge = np.zeros((2, 512, 4, 2, 32))
    for sigma in range(8):
        assert np.allclose(parity[sigma], parity[sigma][0] * along)
        for code in range(8):
            shift = np.exp(2j * math.pi * (signs(sigma) * H4 / 2) @ child_step(code))
            both = (turn @ child_matrix(code)) * shift[None, :] * parity[sigma][0] * -1.0
            half = merge[sigma % 2]
            real, imag = lane_of(code, 0), lane_of(code, 1)
            half[real, sigma // 2, 0, :27] = both.real.T
            half[real, sigma // 2, 1, :27] = both.imag.T
            half[imag, sigma // 2, 0, :27] = -both.imag.T
            half[imag, sigma // 2, 1, :27] = both.real.T
    merge = merge.reshape(2, 512, 256)
    later = np.zeros((2, 4, 56, 8, 2, 32))
    for tau in range(8):
        spot = (signs(tau) * H5 / 2)[:, None] + H6 / 2 * places
        for a in range(8):
            shift = np.exp(2j * math.pi * (signs(a) * W5) @ spot) * along[a]
            both = child_matrix(tau).T * shift[:, None]
            block = later[tau % 2, tau // 2]
            block[:27, a, 0, :27] = both.real
            block[:27, a, 1, :27] = -both.imag
            block[27:54, a, 0, :27] = both.imag
            block[27:54, a, 1, :27] = both.real
    later = later.reshape(448, 512)
    radius = np.zeros((4, 2, 2, 2, 2, 4, 2, 4, 128))
    steps = np.zeros((4, 4, 128))
    for code in range(8):
        bx, by, bz = child_bits(code)
        offset = child_step(code)
        for part in range(2):
            lanes = lane_of(code, part) % 128
            steps[:3, bx * 2 + bz, lanes] = offset
            for qx, qyhi, ax, qylo, ay, az, qz in np.ndindex(4, 2, 2, 2, 2, 2, 4):
                q = np.array([qx, 2 * qyhi + qylo, qz])
                center = -NK / 2 + (2 * q + np.array([ax, ay, az]) + 0.5) * W5
                anchor = -NK / 2 + (q + 0.5) * W6
                node = center[:, None] + offset
                radius[qx, qyhi, ax, qylo, ay, bx * 2 + bz, az, qz, lanes] = np.sqrt(
                    (node**2).sum(0)
                ) - np.sqrt((anchor**2).sum())
    steps[3, :, 64:] = -0.25
    return merge, later, radius.reshape(4, 2, 2, 4, 4, 8, 128), steps


@functools.cache
def cosine_terms():
    nodes = np.cos((np.arange(400) + 0.5) * math.pi / 400) * 0.125 + 0.125
    fitted = np.polynomial.Polynomial.fit(nodes, np.cos(2 * math.pi * np.sqrt(nodes)), 7)
    return [float(c) for c in fitted.convert().coef]


def cosine_of_turns(turns):
    turns = turns - jnp.round(turns)
    square = turns * turns
    terms = cosine_terms()
    total = terms[-1]
    for term in terms[-2::-1]:
        total = total * square + term
    return total


def halves_of(matrix):
    wide = np.asarray(matrix, np.float32)
    high = wide.astype(jnp.bfloat16)
    low = (wide - high.astype(np.float32)).astype(jnp.bfloat16)
    return high, low


def split(x):
    high = x.astype(BF16)
    return high, (x - high.astype(F32)).astype(BF16)


def window_kernel(
    w_ref, box_ref, speed_ref, radius_ref, steps_ref, merge_ref, later_ref, out_ref,
    taken, turned, chunks, got, radius, steps, merge, later, wave, rows,
    mid, other, columns, total, done,
    take_sem, table_sem, send_sem, recv_sem, swap_send, swap_recv, done_sem,
):
    gx, gy, gz = lax.axis_index("gx"), lax.axis_index("gy"), lax.axis_index("gz")
    z, y, x, core = gx // 4, gx % 4, gy // 2, gy % 2
    ax, high = gx // 2 % 2, gy // 4
    place = gy // 2 % 2 * 2 + core
    block = gx % 2 * 2 + gz
    even = lax.rem(high + z, 2)
    inside = even == gz
    beside = lax.rem(z + 3 - 2 * gz, 4)
    side_high = lax.rem(gz + z, 2)
    groups = [(z, side_high), (lax.rem(z + 2, 4), side_high), (beside, 0), (beside, 1)]

    barrier = pltpu.get_barrier_semaphore()

    def tell(to_z, to_y, to_x, to_core, to_gz):
        pl.semaphore_signal(
            barrier,
            inc=1,
            device_id=(to_z * 4 + to_y, to_x * 2 + to_core, to_gz),
            device_id_type=MESH,
        )

    x_low = lax.rem(x, 2)

    @pl.when(jnp.logical_not(inside))
    def _():
        tell(z, y, 2 * side_high + x_low, core, gz)
        tell(z, y, x, core, 1 - gz)

    tell(z, y, 2 * side_high + x_low, core, 1 - gz)
    for number, (to_z, to_high) in enumerate(groups):
        for more in range(4):
            for flip in range(2):
                if number + more > 0:
                    tell(
                        to_z, lax.rem(y + more, 4), 2 * to_high + x_low, core,
                        lax.rem(gz + flip, 2),
                    )

    def tell_all(step, carry):
        to_low = lax.rem(x + step, 2)
        to_core = lax.rem(core + step // 2, 2)
        for to_z, to_high in groups:
            for more in range(4):
                for flip in range(2):
                    tell(
                        to_z, lax.rem(y + more, 4), 2 * to_high + to_low, to_core,
                        lax.rem(gz + flip, 2),
                    )
        return carry

    lax.fori_loop(1, 4, tell_all, 0)

    takes = [
        pltpu.make_async_copy(
            w_ref.at[:, half * 128 : half * 128 + 128], taken.at[half], take_sem.at[half]
        )
        for half in range(2)
    ]
    sources = [(steps_ref, steps), (merge_ref, merge), (later_ref, later)]
    sources += [(radius_ref.at[qx, qy], radius.at[k]) for k, (qx, qy) in enumerate(groups)]
    fetches = [
        pltpu.make_async_copy(source, target, table_sem.at[number])
        for number, (source, target) in enumerate(sources)
    ]
    for copy in takes + fetches:
        copy.start()
    turned[...] = jnp.zeros_like(turned)
    for half in range(2):
        takes[half].wait()
        for row in range(7):
            depth = row % 4 * 2 + row // 4
            turned[0:54, :] = taken.at[half][pl.ds(depth, 54, stride=8), :]
            turned[64:118, :] = taken.at[half][pl.ds(432 + depth, 54, stride=8), :]
            if row < 6:
                last = 72 * row + 7
                turned[54:63, :] = taken.at[half][pl.ds(432 + last, 9, stride=8), :]
                turned[118:127, :] = taken.at[half][pl.ds(last, 9, stride=8), :]
            chunks[pl.ds(half * 1024 + row, 128, stride=8), :] = turned[...].T

    first = (gx * 8 + gy) * 2
    real_side = lax.broadcasted_iota(jnp.int32, (8, 128), 1) < 64
    upper = lax.broadcasted_iota(jnp.int32, (8, 128), 0) < 4

    def make_wave(which):
        start = steps[3]
        for axis in range(3):
            center = (box_ref[axis, first + which].astype(F32) + 0.5) / TG - 0.5
            part = steps[axis] * center
            start = start + (part - jnp.round(part))
        start = (start - jnp.round(start))[None, :, None, :]
        speed = speed_ref[first + which]

        def make(number, carry):
            value = cosine_of_turns(radius[number // 2, number % 2] * speed + start)
            over = pltpu.roll(value, 64, 3)
            wave[0, which, number % 2, number // 2] = jnp.where(real_side, value, over)
            wave[1, which, number % 2, number // 2] = jnp.where(real_side, -over, value)
            return carry

        lax.fori_loop(0, 8, make, 0)

    fetches[0].wait()
    for fetch in fetches[3:]:
        fetch.wait()
    make_wave(0)
    pl.semaphore_wait(barrier, 128)

    def chunk(to_gx, to_gy, which):
        return chunks.at[pl.ds(pl.multiple_of((to_gx * 8 + to_gy) * 16 + which * 8, 8), 7)]

    def send(more, to_y, to_x, to_core, which, turn):
        to_gx, to_gy = lax.rem(z + more, 4) * 4 + to_y, to_x * 2 + to_core
        slot = (0, 2 + high, 1, 2 + high)[more]
        layer = (even, 0, even, 1)[more]
        pltpu.make_async_remote_copy(
            chunk(to_gx, to_gy, which),
            got.at[which, ax, slot * 4 + place, block, 0:7],
            send_sem,
            recv_sem.at[which, turn],
            device_id=(to_gx, to_gy, layer),
            device_id_type=MESH,
        ).start()

    for which in range(2):
        for turn in range(2):
            to_core = lax.rem(ax + turn, 2)
            itself = jnp.logical_and(inside, to_core == core)

            @pl.when(itself)
            def _():
                pltpu.make_async_copy(
                    chunk(gx, gy, which),
                    got.at[which, ax, place, block, 0:7],
                    recv_sem.at[which, turn],
                ).start()

            @pl.when(jnp.logical_not(itself))
            def _():
                send(0, y, x, to_core, which, turn)

            for more in range(1, 4):
                send(more, y, x, to_core, which, turn)

            def send_all(step, carry):
                to_x = lax.rem(x + step, 4)
                to_y = lax.rem(y + step // 4, 4)
                for more in range(4):
                    send(more, to_y, to_x, to_core, which, turn)
                return carry

            lax.fori_loop(1, 16, send_all, 0)

    make_wave(1)
    fetches[1].wait()
    fetches[2].wait()
    sublane = lax.broadcasted_iota(jnp.int32, (8, 128), 0)
    entry = lax.broadcasted_iota(jnp.int32, (8, 128), 1) % 64
    packed = (sublane < 6) & (entry >= 9 * sublane) & (entry < 9 * sublane + 9)
    lane_low = lax.broadcasted_iota(jnp.int32, (64, 128), 1) < 64
    first_side = lax.broadcasted_iota(jnp.int32, (56, 128), 1) < 64

    def swap(which, turn):
        part = lax.rem(turn + core, 2)
        return pltpu.make_async_remote_copy(
            other.at[which, part],
            mid.at[gz, which, part],
            swap_send.at[which, turn],
            swap_recv.at[which, turn],
            device_id=(gx, gy, 1 - gz),
            device_id_type=MESH,
        )

    def merge_part(which, turn):
        part = lax.rem(turn + core, 2)
        landed = got.at[which, part, :, :, 0:7]
        pltpu.make_async_copy(landed, landed, recv_sem.at[which, turn]).wait()

        def group(slot, carry):
            for ay in range(2):
                row = pl.multiple_of(ay * 64 + slot * 8, 8)
                for side in range(4):
                    pair = []
                    for low in range(2):
                        at = 2 * low + ay
                        value = got[which, part, slot * 4 + at, side]
                        moved = pltpu.roll(value, 10, 1, stride=9, stride_axis=0)
                        moved = jnp.where(packed, moved, 0.0)
                        last = jnp.sum(moved, axis=0, keepdims=True)
                        value = jnp.where(sublane == 7, last, value)
                        pair.append(
                            value * wave[0, which, part, slot, at, side]
                            + pltpu.roll(value, 64, 1) * wave[1, which, part, slot, at, side]
                        )
                    lanes = slice(side * 128, side * 128 + 128)
                    rows[pl.ds(row, 8), lanes] = jnp.where(
                        upper, pair[0], pltpu.roll(pair[1], 4, 0)
                    )
                    rows[pl.ds(row + 32, 8), lanes] = jnp.where(
                        upper, pltpu.roll(pair[0], 4, 0), pair[1]
                    )
            return carry

        lax.fori_loop(0, 4, group, 0)
        high_rows, low_rows = split(rows[...])
        both_rows = jnp.concatenate([high_rows, low_rows], axis=0)

        def product(side):
            out = jnp.dot(both_rows, merge[0, side], preferred_element_type=F32)
            rest = jnp.dot(high_rows, merge[1, side], preferred_element_type=F32)
            return out[:128] + out[128:] + rest

        other[which, part] = product(1 - gz)
        swap(which, turn).start()
        mid[gz, which, part] = product(gz)

    def leave(number):
        return pltpu.make_async_copy(
            done.at[number].reshape(54, 2, 128),
            out_ref.at[:, :, number * 128 : number * 128 + 128],
            done_sem.at[number],
        )

    def later_part(which, turn):
        part = lax.rem(turn + core, 2)
        swap(which, turn).wait()
        for couple in range(2):
            stacked = []
            for a in (2 * couple, 2 * couple + 1):
                pieces = []
                for qx in range(4):
                    away = lax.rem(qx + 4 - z, 4)
                    odd = lax.rem(away, 2)
                    for qy in range(2):
                        owner = (1 - odd) * ((qx + qy) % 2) + odd * (1 - away // 2)
                        slot = (1 - odd) * (away // 2) + odd * (2 + qy)
                        at = pl.multiple_of(a * 32 + slot * 8, 8)
                        pieces.append(mid[owner, which, part, pl.ds(at, 8), :])
                stacked.append(jnp.concatenate(pieces, axis=0))
            for sigma_x in range(2):
                lanes = slice(sigma_x * 128, sigma_x * 128 + 128)
                even, odd = stacked[0][:, lanes], stacked[1][:, lanes]
                both = jnp.concatenate(
                    [
                        jnp.where(lane_low, even, pltpu.roll(odd, 64, 1)),
                        jnp.where(lane_low, pltpu.roll(even, 64, 1), odd),
                    ],
                    axis=0,
                )
                columns[couple * 128 : couple * 128 + 128, lanes] = both.T
        high_part, low_part = split(columns[...])
        result = jnp.dot(later[part], high_part, preferred_element_type=F32)
        result = result[:448] + result[448:]
        result += jnp.dot(later[part, :448], low_part, preferred_element_type=F32)
        if turn == 0:
            total[...] = result
            return
        result = result + total[...]
        for sigma_x in range(2):
            lanes = slice(sigma_x * 128, sigma_x * 128 + 128)
            for tau in range(4):
                down = result[tau * 56 : tau * 56 + 56, lanes]
                up = result[224 + tau * 56 : 224 + tau * 56 + 56, lanes]
                number = sigma_x * 8 + tau
                done.at[number][pl.ds(which, 54, stride=2), :] = jnp.where(
                    first_side, down, pltpu.roll(up, 64, 1)
                )[:54]
                done.at[number + 4][pl.ds(which, 54, stride=2), :] = jnp.where(
                    first_side, pltpu.roll(down, 64, 1), up
                )[:54]
                if which == 1:
                    leave(number).start()
                    leave(number + 4).start()

    merge_part(0, 0)
    merge_part(0, 1)
    later_part(0, 0)
    merge_part(1, 0)
    later_part(0, 1)
    merge_part(1, 1)
    later_part(1, 0)
    later_part(1, 1)
    for number in range(16):
        leave(number).wait()

    @pl.when(inside)
    def _():
        rest = chunks.at[pl.ds(0, 254 * 7)]
        pltpu.make_async_copy(rest, rest, send_sem).wait()

    @pl.when(jnp.logical_not(inside))
    def _():
        rest = chunks.at[pl.ds(0, 256 * 7)]
        pltpu.make_async_copy(rest, rest, send_sem).wait()


SMEM = pl.BlockSpec(memory_space=pltpu.SMEM)
ANY = pl.BlockSpec(memory_space=pl.ANY)


def per_device(weights, target_box, wave_speed):
    merge, later, radius, steps = tables()
    out = pl.pallas_call(
        window_kernel,
        out_shape=jax.ShapeDtypeStruct((54, 2, 2048), F32),
        in_specs=[ANY, SMEM, SMEM, ANY, ANY, ANY, ANY],
        out_specs=ANY,
        scratch_shapes=[
            pltpu.VMEM((3, 864, 128), F32),
            pltpu.VMEM((128, 128), F32),
            pltpu.VMEM((2048, 128), F32),
            pltpu.VMEM((2, 2, 16, 4, 8, 128), F32),
            pltpu.VMEM((4, 2, 4, 4, 8, 128), F32),
            pltpu.VMEM((4, 4, 128), F32),
            pltpu.VMEM((2, 2, 512, 256), BF16),
            pltpu.VMEM((2, 896, 256), BF16),
            pltpu.VMEM((2, 2, 2, 4, 4, 4, 8, 128), F32),
            pltpu.VMEM((128, 512), F32),
            pltpu.VMEM((2, 2, 2, 128, 256), F32),
            pltpu.VMEM((2, 2, 128, 256), F32),
            pltpu.VMEM((256, 256), F32),
            pltpu.VMEM((448, 256), F32),
            pltpu.VMEM((17, 108, 128), F32),
            pltpu.SemaphoreType.DMA((2,)),
            pltpu.SemaphoreType.DMA((7,)),
            pltpu.SemaphoreType.DMA,
            pltpu.SemaphoreType.DMA((2, 2)),
            pltpu.SemaphoreType.DMA((2, 2)),
            pltpu.SemaphoreType.DMA((2, 2)),
            pltpu.SemaphoreType.DMA((16,)),
        ],
        compiler_params=pltpu.CompilerParams(
            collective_id=0, has_side_effects=True, vmem_limit_bytes=58 * 2**20
        ),
        name="window",
    )(
        weights.reshape(864, 256),
        target_box,
        wave_speed,
        jnp.asarray(radius, F32),
        jnp.asarray(steps, F32),
        jnp.asarray(np.stack(halves_of(merge))),
        jnp.asarray(np.concatenate(halves_of(later.reshape(448, 2, 256).swapaxes(0, 1)), axis=1)),
    )
    return out.reshape(2, 27, 1, 2, 2048)


def solution(mesh):
    return jax.shard_map(
        per_device,
        mesh=mesh,
        in_specs=(P(None, None, "gx", "gy", "gz", None, None), P(), P()),
        out_specs=P(None, None, "gz", ("gx", "gy"), None),
        check_vma=False,
    )
```

```python
import functools
import math

import jax
import jax.numpy as jnp
import numpy as np
from jax import lax
from jax.experimental import pallas as pl
from jax.experimental.pallas import tpu as pltpu
from jax.sharding import PartitionSpec as P

TG = 16
NK = 256.0
MESH = pl.DeviceIdType.MESH
F32 = jnp.float32
BF16 = jnp.bfloat16


def chebyshev_points():
    return np.array([-math.sqrt(3.0) / 2.0, 0.0, math.sqrt(3.0) / 2.0])


def node_places():
    points = chebyshev_points()
    numbers = np.arange(27)
    return np.stack([points[numbers // 9], points[numbers // 3 % 3], points[numbers % 3]])


def lagrange_line(child_bit):
    points = chebyshev_points()
    places = child_bit - 0.5 + points / 2.0
    lagrange = np.ones((3, 3))
    for parent_node in range(3):
        for others in range(3):
            if others != parent_node:
                lagrange[parent_node, :] = (
                    lagrange[parent_node, :]
                    * (places - points[others])
                    / (points[parent_node] - points[others])
                )
    return lagrange


def child_bits(code):
    return (code // 4, code // 2 % 2, code % 2)


def child_matrix(code):
    picked = child_bits(code)
    return np.kron(
        np.kron(lagrange_line(picked[0]), lagrange_line(picked[1])), lagrange_line(picked[2])
    )


W4 = NK / 16
W5, W6 = 2 * W4, 4 * W4
H4 = 1.0 / TG
H5, H6 = H4 / 2, H4 / 4


def signs(code):
    return np.array(child_bits(code)) - 0.5


def child_step(code):
    return signs(code)[:, None] * W4 + 0.5 * W4 * node_places()


def lane_of(code, part):
    bx, by, bz = child_bits(code)
    return (bx * 2 + bz) * 128 + part * 64 + 2 * np.arange(27) + by


@functools.cache
def tables():
    places = node_places()
    turn = np.exp(2j * math.pi * H5 * W5 / 4.0 * (places.T @ places))
    parity = {}
    for sigma in range(8):
        row = [np.exp(2j * math.pi * (signs(sigma) * H4 / 2) @ (signs(a) * W5)) for a in range(8)]
        parity[sigma] = np.array(row)
    along = parity[0] / parity[0][0]
    merge = np.zeros((2, 512, 4, 2, 32))
    for sigma in range(8):
        assert np.allclose(parity[sigma], parity[sigma][0] * along)
        for code in range(8):
            shift = np.exp(2j * math.pi * (signs(sigma) * H4 / 2) @ child_step(code))
            both = (turn @ child_matrix(code)) * shift[None, :] * parity[sigma][0] * -1.0
            half = merge[sigma % 2]
            real, imag = lane_of(code, 0), lane_of(code, 1)
            half[real, sigma // 2, 0, :27] = both.real.T
            half[real, sigma // 2, 1, :27] = both.imag.T
            half[imag, sigma // 2, 0, :27] = -both.imag.T
            half[imag, sigma // 2, 1, :27] = both.real.T
    merge = merge.reshape(2, 512, 256)
    later = np.zeros((2, 4, 56, 8, 2, 32))
    for tau in range(8):
        spot = (signs(tau) * H5 / 2)[:, None] + H6 / 2 * places
        for a in range(8):
            shift = np.exp(2j * math.pi * (signs(a) * W5) @ spot) * along[a]
            both = child_matrix(tau).T * shift[:, None]
            block = later[tau % 2, tau // 2]
            block[:27, a, 0, :27] = both.real
            block[:27, a, 1, :27] = -both.imag
            block[27:54, a, 0, :27] = both.imag
            block[27:54, a, 1, :27] = both.real
    later = later.reshape(448, 512)
    radius = np.zeros((4, 2, 2, 2, 2, 4, 2, 4, 128))
    steps = np.zeros((4, 4, 128))
    for code in range(8):
        bx, by, bz = child_bits(code)
        offset = child_step(code)
        for part in range(2):
            lanes = lane_of(code, part) % 128
            steps[:3, bx * 2 + bz, lanes] = offset
            for qx, qyhi, ax, qylo, ay, az, qz in np.ndindex(4, 2, 2, 2, 2, 2, 4):
                q = np.array([qx, 2 * qyhi + qylo, qz])
                center = -NK / 2 + (2 * q + np.array([ax, ay, az]) + 0.5) * W5
                anchor = -NK / 2 + (q + 0.5) * W6
                node = center[:, None] + offset
                radius[qx, qyhi, ax, qylo, ay, bx * 2 + bz, az, qz, lanes] = np.sqrt(
                    (node**2).sum(0)
                ) - np.sqrt((anchor**2).sum())
    steps[3, :, 64:] = -0.25
    return merge, later, radius.reshape(4, 2, 2, 4, 4, 8, 128), steps


@functools.cache
def cosine_terms():
    nodes = np.cos((np.arange(400) + 0.5) * math.pi / 400) * 0.125 + 0.125
    fitted = np.polynomial.Polynomial.fit(nodes, np.cos(2 * math.pi * np.sqrt(nodes)), 7)
    return [float(c) for c in fitted.convert().coef]


def cosine_of_turns(turns):
    turns = turns - jnp.round(turns)
    square = turns * turns
    terms = cosine_terms()
    total = terms[-1]
    for term in terms[-2::-1]:
        total = total * square + term
    return total


def halves_of(matrix):
    wide = np.asarray(matrix, np.float32)
    high = wide.astype(jnp.bfloat16)
    low = (wide - high.astype(np.float32)).astype(jnp.bfloat16)
    return high, low


def split(x):
    high = x.astype(BF16)
    return high, (x - high.astype(F32)).astype(BF16)


def window_kernel(
    w_ref, box_ref, speed_ref, radius_ref, steps_ref, merge_ref, later_ref, out_ref,
    taken, turned, chunks, got, radius, steps, merge, later, wave, rows,
    mid, other, columns, total, done,
    take_sem, table_sem, send_sem, recv_sem, swap_send, swap_recv, done_sem,
):
    gx, gy, gz = lax.axis_index("gx"), lax.axis_index("gy"), lax.axis_index("gz")
    z, y, x, core = gx // 4, gx % 4, gy // 2, gy % 2
    ax, high = gx // 2 % 2, gy // 4
    place = gy // 2 % 2 * 2 + core
    block = gx % 2 * 2 + gz
    even = lax.rem(high + z, 2)
    inside = even == gz
    beside = lax.rem(z + 3 - 2 * gz, 4)
    side_high = lax.rem(gz + z, 2)
    groups = [(z, side_high), (lax.rem(z + 2, 4), side_high), (beside, 0), (beside, 1)]

    barrier = pltpu.get_barrier_semaphore()

    def tell(to_z, to_y, to_x, to_core, to_gz):
        pl.semaphore_signal(
            barrier,
            inc=1,
            device_id=(to_z * 4 + to_y, to_x * 2 + to_core, to_gz),
            device_id_type=MESH,
        )

    x_low = lax.rem(x, 2)

    @pl.when(jnp.logical_not(inside))
    def _():
        tell(z, y, 2 * side_high + x_low, core, gz)
        tell(z, y, x, core, 1 - gz)

    tell(z, y, 2 * side_high + x_low, core, 1 - gz)
    for number, (to_z, to_high) in enumerate(groups):
        for more in range(4):
            for flip in range(2):
                if number + more > 0:
                    tell(
                        to_z, lax.rem(y + more, 4), 2 * to_high + x_low, core,
                        lax.rem(gz + flip, 2),
                    )

    def tell_all(step, carry):
        to_low = lax.rem(x + step, 2)
        to_core = lax.rem(core + step // 2, 2)
        for to_z, to_high in groups:
            for more in range(4):
                for flip in range(2):
                    tell(
                        to_z, lax.rem(y + more, 4), 2 * to_high + to_low, to_core,
                        lax.rem(gz + flip, 2),
                    )
        return carry

    lax.fori_loop(1, 4, tell_all, 0)

    takes = [
        pltpu.make_async_copy(
            w_ref.at[:, half * 128 : half * 128 + 128], taken.at[half], take_sem.at[half]
        )
        for half in range(2)
    ]
    sources = [(steps_ref, steps), (merge_ref, merge), (later_ref, later)]
    sources += [(radius_ref.at[qx, qy], radius.at[k]) for k, (qx, qy) in enumerate(groups)]
    fetches = [
        pltpu.make_async_copy(source, target, table_sem.at[number])
        for number, (source, target) in enumerate(sources)
    ]
    for copy in takes + fetches:
        copy.start()
    turned[...] = jnp.zeros_like(turned)
    for half in range(2):
        takes[half].wait()
        for row in range(7):
            depth = row % 4 * 2 + row // 4
            turned[0:54, :] = taken.at[half][pl.ds(depth, 54, stride=8), :]
            turned[64:118, :] = taken.at[half][pl.ds(432 + depth, 54, stride=8), :]
            if row < 6:
                last = 72 * row + 7
                turned[54:63, :] = taken.at[half][pl.ds(432 + last, 9, stride=8), :]
                turned[118:127, :] = taken.at[half][pl.ds(last, 9, stride=8), :]
            chunks[pl.ds(half * 1024 + row, 128, stride=8), :] = turned[...].T

    first = (gx * 8 + gy) * 2
    real_side = lax.broadcasted_iota(jnp.int32, (8, 128), 1) < 64
    upper = lax.broadcasted_iota(jnp.int32, (8, 128), 0) < 4

    def make_wave(which):
        start = steps[3]
        for axis in range(3):
            center = (box_ref[axis, first + which].astype(F32) + 0.5) / TG - 0.5
            part = steps[axis] * center
            start = start + (part - jnp.round(part))
        start = (start - jnp.round(start))[None, :, None, :]
        speed = speed_ref[first + which]

        def make(number, carry):
            value = cosine_of_turns(radius[number // 2, number % 2] * speed + start)
            over = pltpu.roll(value, 64, 3)
            wave[0, which, number % 2, number // 2] = jnp.where(real_side, value, over)
            wave[1, which, number % 2, number // 2] = jnp.where(real_side, -over, value)
            return carry

        lax.fori_loop(0, 8, make, 0)

    fetches[0].wait()
    for fetch in fetches[3:]:
        fetch.wait()
    make_wave(0)
    pl.semaphore_wait(barrier, 128)

    def chunk(to_gx, to_gy, which):
        return chunks.at[pl.ds(pl.multiple_of((to_gx * 8 + to_gy) * 16 + which * 8, 8), 7)]

    def send(more, to_y, to_x, to_core, which, turn):
        to_gx, to_gy = lax.rem(z + more, 4) * 4 + to_y, to_x * 2 + to_core
        slot = (0, 2 + high, 1, 2 + high)[more]
        layer = (even, 0, even, 1)[more]
        pltpu.make_async_remote_copy(
            chunk(to_gx, to_gy, which),
            got.at[which, ax, slot * 4 + place, block, 0:7],
            send_sem,
            recv_sem.at[which, turn],
            device_id=(to_gx, to_gy, layer),
            device_id_type=MESH,
        ).start()

    for which in range(2):
        for turn in range(2):
            to_core = lax.rem(ax + turn, 2)
            itself = jnp.logical_and(inside, to_core == core)

            @pl.when(itself)
            def _():
                pltpu.make_async_copy(
                    chunk(gx, gy, which),
                    got.at[which, ax, place, block, 0:7],
                    recv_sem.at[which, turn],
                ).start()

            @pl.when(jnp.logical_not(itself))
            def _():
                send(0, y, x, to_core, which, turn)

            for more in range(1, 4):
                send(more, y, x, to_core, which, turn)

            def send_all(step, carry):
                to_x = lax.rem(x + step, 4)
                to_y = lax.rem(y + step // 4, 4)
                for more in range(4):
                    send(more, to_y, to_x, to_core, which, turn)
                return carry

            lax.fori_loop(1, 16, send_all, 0)

    make_wave(1)
    fetches[1].wait()
    fetches[2].wait()
    sublane = lax.broadcasted_iota(jnp.int32, (8, 128), 0)
    entry = lax.broadcasted_iota(jnp.int32, (8, 128), 1) % 64
    packed = (sublane < 6) & (entry >= 9 * sublane) & (entry < 9 * sublane + 9)
    lane_low = lax.broadcasted_iota(jnp.int32, (64, 128), 1) < 64
    first_side = lax.broadcasted_iota(jnp.int32, (56, 128), 1) < 64

    def swap(which, turn):
        part = lax.rem(turn + core, 2)
        return pltpu.make_async_remote_copy(
            other.at[which, part],
            mid.at[gz, which, part],
            swap_send.at[which, turn],
            swap_recv.at[which, turn],
            device_id=(gx, gy, 1 - gz),
            device_id_type=MESH,
        )

    def merge_part(which, turn):
        part = lax.rem(turn + core, 2)
        landed = got.at[which, part, :, :, 0:7]
        pltpu.make_async_copy(landed, landed, recv_sem.at[which, turn]).wait()

        def group(slot, carry):
            for ay in range(2):
                row = pl.multiple_of(ay * 64 + slot * 8, 8)
                for side in range(4):
                    pair = []
                    for low in range(2):
                        at = 2 * low + ay
                        value = got[which, part, slot * 4 + at, side]
                        moved = pltpu.roll(value, 10, 1, stride=9, stride_axis=0)
                        moved = jnp.where(packed, moved, 0.0)
                        last = jnp.sum(moved, axis=0, keepdims=True)
                        value = jnp.where(sublane == 7, last, value)
                        pair.append(
                            value * wave[0, which, part, slot, at, side]
                            + pltpu.roll(value, 64, 1) * wave[1, which, part, slot, at, side]
                        )
                    lanes = slice(side * 128, side * 128 + 128)
                    rows[pl.ds(row, 8), lanes] = jnp.where(
                        upper, pair[0], pltpu.roll(pair[1], 4, 0)
                    )
                    rows[pl.ds(row + 32, 8), lanes] = jnp.where(
                        upper, pltpu.roll(pair[0], 4, 0), pair[1]
                    )
            return carry

        for slot in range(4):
            group(slot, 0)
        high_rows, low_rows = split(rows[...])
        both_rows = jnp.concatenate([high_rows, low_rows], axis=0)

        def product(side):
            out = jnp.dot(both_rows, merge[0, side], preferred_element_type=F32)
            rest = jnp.dot(high_rows, merge[1, side], preferred_element_type=F32)
            return out[:128] + out[128:] + rest

        other[which, part] = product(1 - gz)
        swap(which, turn).start()
        mid[gz, which, part] = product(gz)

    def leave(which, number):
        return pltpu.make_async_copy(
            done.at[which, number],
            out_ref.at[:, which, number * 128 : number * 128 + 128],
            done_sem.at[which, number],
        )

    def later_part(which, turn):
        part = lax.rem(turn + core, 2)
        swap(which, turn).wait()
        for couple in range(2):
            stacked = []
            for a in (2 * couple, 2 * couple + 1):
                pieces = []
                for qx in range(4):
                    away = lax.rem(qx + 4 - z, 4)
                    odd = lax.rem(away, 2)
                    for qy in range(2):
                        owner = (1 - odd) * ((qx + qy) % 2) + odd * (1 - away // 2)
                        slot = (1 - odd) * (away // 2) + odd * (2 + qy)
                        at = pl.multiple_of(a * 32 + slot * 8, 8)
                        pieces.append(mid[owner, which, part, pl.ds(at, 8), :])
                stacked.append(jnp.concatenate(pieces, axis=0))
            for sigma_x in range(2):
                lanes = slice(sigma_x * 128, sigma_x * 128 + 128)
                even, odd = stacked[0][:, lanes], stacked[1][:, lanes]
                both = jnp.concatenate(
                    [
                        jnp.where(lane_low, even, pltpu.roll(odd, 64, 1)),
                        jnp.where(lane_low, pltpu.roll(even, 64, 1), odd),
                    ],
                    axis=0,
                )
                columns[couple * 128 : couple * 128 + 128, lanes] = both.T
        high_part, low_part = split(columns[...])
        result = jnp.dot(later[part], high_part, preferred_element_type=F32)
        result = result[:448] + result[448:]
        result += jnp.dot(later[part, :448], low_part, preferred_element_type=F32)
        if turn == 0:
            total[...] = result
            return
        result = result + total[...]
        for sigma_x in range(2):
            lanes = slice(sigma_x * 128, sigma_x * 128 + 128)
            for tau in range(4):
                down = result[tau * 56 : tau * 56 + 56, lanes]
                up = result[224 + tau * 56 : 224 + tau * 56 + 56, lanes]
                number = sigma_x * 8 + tau
                done[which, number] = jnp.where(
                    first_side, down, pltpu.roll(up, 64, 1)
                )[:54]
                done[which, number + 4] = jnp.where(
                    first_side, pltpu.roll(down, 64, 1), up
                )[:54]
                leave(which, number).start()
                leave(which, number + 4).start()

    merge_part(0, 0)
    merge_part(0, 1)
    later_part(0, 0)
    merge_part(1, 0)
    merge_part(1, 1)
    later_part(0, 1)
    later_part(1, 0)
    later_part(1, 1)
    for which in range(2):
        for number in range(16):
            leave(which, number).wait()

    @pl.when(inside)
    def _():
        rest = chunks.at[pl.ds(0, 254 * 7)]
        pltpu.make_async_copy(rest, rest, send_sem).wait()

    @pl.when(jnp.logical_not(inside))
    def _():
        rest = chunks.at[pl.ds(0, 256 * 7)]
        pltpu.make_async_copy(rest, rest, send_sem).wait()


SMEM = pl.BlockSpec(memory_space=pltpu.SMEM)
ANY = pl.BlockSpec(memory_space=pl.ANY)


def per_device(weights, target_box, wave_speed):
    merge, later, radius, steps = tables()
    out = pl.pallas_call(
        window_kernel,
        out_shape=jax.ShapeDtypeStruct((54, 2, 2048), F32),
        in_specs=[ANY, SMEM, SMEM, ANY, ANY, ANY, ANY],
        out_specs=ANY,
        scratch_shapes=[
            pltpu.VMEM((3, 864, 128), F32),
            pltpu.VMEM((128, 128), F32),
            pltpu.VMEM((2048, 128), F32),
            pltpu.VMEM((2, 2, 16, 4, 8, 128), F32),
            pltpu.VMEM((4, 2, 4, 4, 8, 128), F32),
            pltpu.VMEM((4, 4, 128), F32),
            pltpu.VMEM((2, 2, 512, 256), BF16),
            pltpu.VMEM((2, 896, 256), BF16),
            pltpu.VMEM((2, 2, 2, 4, 4, 4, 8, 128), F32),
            pltpu.VMEM((128, 512), F32),
            pltpu.VMEM((2, 2, 2, 128, 256), F32),
            pltpu.VMEM((2, 2, 128, 256), F32),
            pltpu.VMEM((256, 256), F32),
            pltpu.VMEM((448, 256), F32),
            pltpu.VMEM((2, 16, 54, 128), F32),
            pltpu.SemaphoreType.DMA((2,)),
            pltpu.SemaphoreType.DMA((7,)),
            pltpu.SemaphoreType.DMA,
            pltpu.SemaphoreType.DMA((2, 2)),
            pltpu.SemaphoreType.DMA((2, 2)),
            pltpu.SemaphoreType.DMA((2, 2)),
            pltpu.SemaphoreType.DMA((2, 16)),
        ],
        compiler_params=pltpu.CompilerParams(
            collective_id=0, has_side_effects=True, vmem_limit_bytes=58 * 2**20
        ),
        name="window",
    )(
        weights.reshape(864, 256),
        target_box,
        wave_speed,
        jnp.asarray(radius, F32),
        jnp.asarray(steps, F32),
        jnp.asarray(np.stack(halves_of(merge))),
        jnp.asarray(np.concatenate(halves_of(later.reshape(448, 2, 256).swapaxes(0, 1)), axis=1)),
    )
    return out.reshape(2, 27, 1, 2, 2048)


def solution(mesh):
    return jax.shard_map(
        per_device,
        mesh=mesh,
        in_specs=(P(None, None, "gx", "gy", "gz", None, None), P(), P()),
        out_specs=P(None, None, "gz", ("gx", "gy"), None),
        check_vma=False,
    )
```
